32 devices in a mesh: groups: 2 (over x), expert: 16 (over z, y, core), learner: 1.
Axes of the slice: x: 2, y: 2, z: 4, core: 2. Of those that a mesh axis runs over, the one named last changes fastest.
Arguments:
- hidden_act: bfloat16 [2, 512, 8, 1024], P(None, ('groups', 'expert', 'learner')), parts along dimension 1, may hold values from -6 to 6
- routes: int32 [2, 512, 8], P(None, ('groups', 'expert', 'learner')), parts along dimension 1, may hold values from 0 to 15, all different within a row; in each aligned block of 16 rows (0 to 15, 16 to 31, ..., all dimensions but the last counted through in order) at most 12 rows name the same one
- gates: float32 [2, 512, 8], P(None, ('groups', 'expert', 'learner')), parts along dimension 1, may hold values from 0.1 to 1
- down_codes: bfloat16 [16, 1024, 7168], P('expert', None, 'learner')
- down_scales: float32 [16, 8, 56], P('expert', None, 'learner'), may hold values from 0.01 to 0.05
- changed: int32 [32], P('groups'), parts along dimension 0, may hold values from 0 to 15, as said below
- fresh_codes: bfloat16 [32, 1, 448, 128, 128], P('groups', 'learner', 'expert'), parts along dimension 0
- fresh_scales: float32 [32, 1, 448], P('groups', 'learner', 'expert'), parts along dimension 0, may hold values from 0.01 to 0.05
- block_ids: int32 [32, 1, 448], P('groups'), parts along dimension 0, may hold values from 0 to 447, each once within a row
Outputs:
- layer_out: bfloat16 [2, 512, 7168], P(None, ('groups', 'expert', 'learner')), parts along dimension 1
The draws below stay inside these ranges and needn't reach their ends.
There are 2 independent parts, one for each index of `groups`. The reference program is written for one: setup_inputs(seed, part) draws one part's arguments, and reference() takes and returns one part's arrays. A program takes and returns all parts, laid end to end along the dimension named above; an argument that names none is the same for every part. Nothing has to cross between parts.
Inputs may be any that keep to these rules, and one draw needn't show every extreme that they name: `routes`: each row names 8 different experts. Within the 16 rows that one device holds in one step, no expert is named more than 12 times, a bound that some block reaches. `changed`: 16 different experts. `block_ids`: for each changed expert and column half, every block position appears once.
All inputs are finite; a program needn't handle non-finite values.
Results may differ from the reference program's by a relative error of at most 0.0057.
Values may be sent and summed in bfloat16 or wider, within the bound.
No kernel may reach another device: no remote copies, remote signals or barrier semaphores. Data moves between devices by JAX's collectives and lax.ppermute only.
A program may use at most 192 MiB of HBM per device.

```python
import math
import jax
import jax.numpy as jnp
import numpy as np
from jax import lax

D = 7168
FW = 1024
BLK = 128
TOPK = 8
STEPS = 2
CHANGED = 16
ROWS_DEV = 16
E = 16
ROWS = 256
CAP = 12
BPH = 448
N_EXPERT = 16
N_LEARNER = 1


def code_values(key, grid_shape):
    drawn = jax.random.randint(key, grid_shape, 0, 80)
    mantissa = (drawn % 8).astype(jnp.float32)
    level = drawn // 8
    exponent = (level % 5 - 3).astype(jnp.float32)
    signs = (level // 5 * 2 - 1).astype(jnp.float32)
    return signs * (1.0 + mantissa / 8.0) * jnp.exp2(exponent)


def draw_down_codes(key, part):
    key = jax.random.fold_in(key, 21)
    return code_values(key, (E, FW, D)).astype(jnp.bfloat16)


def draw_fresh_codes(key, part):
    key = jax.random.fold_in(key, 37)
    return code_values(key, (CHANGED, N_LEARNER, BPH, BLK, BLK)).astype(jnp.bfloat16)


def draw_changed(key, part):
    key = jax.random.fold_in(key, 53)
    order = jax.random.permutation(key, E)
    return order[:CHANGED].astype(jnp.int32)


def level_of(own_key, dims, pieces, least, top_value):
    loudness = 1.0
    for dim, blocks in pieces:
        draws = jax.random.uniform(jax.random.fold_in(jax.random.fold_in(own_key, 6), dim), (blocks,), jnp.float32, least / len(pieces), top_value / len(pieces))
        loudness = loudness * jnp.repeat(jnp.exp(draws), dims[dim] // blocks).reshape((-1,) + (1,) * (len(dims) - 1 - dim))
    return loudness


def deal_out(stream_key, own, number, rows, number_of, top, most, lean):
    sequence = jax.random.permutation(stream_key, number_of)
    crowded, common = load_shares(number_of, rows * top, most, lean, True), load_shares(number_of, rows * top, most, lean, False)
    places = jnp.arange(number_of)

    def named(tallies, rotation):
        used = int((tallies > 0).sum())
        fixed = max(1, used // 4)
        passed = fixed + (places - fixed + rotation * (used - fixed)) % max(1, number_of - fixed)
        return jnp.zeros((number_of,), jnp.int32).at[sequence[jnp.where(places < fixed, places, passed)]].set(jnp.asarray(tallies, jnp.int32))

    tallies = jnp.where(number % 4 == 0, named(crowded, number // 4), named(common, number - number // 4 - 1))
    mixed = jax.random.permutation(jax.random.fold_in(own, 3), number_of)
    source_of, receiver = mixed[0:number_of // 2 * 2:2], mixed[1:number_of // 2 * 2:2]
    room = jnp.minimum(tallies[source_of] - 1, most - tallies[receiver]) // 2
    room = jnp.where((source_of == sequence[0]) | (receiver == sequence[0]) | (tallies[receiver] == 0), 0, jnp.maximum(room, 0))
    passed = jax.random.randint(jax.random.fold_in(own, 4), (number_of // 2,), 0, 1 << 20) % (room + 1)
    tallies = tallies.at[source_of].add(-passed).at[receiver].add(passed)
    items = jnp.searchsorted(jnp.cumsum(tallies), jnp.arange(rows * top), side="right").astype(jnp.int32)
    grid = items.reshape(top, rows).T
    grid = grid[jax.random.permutation(jax.random.fold_in(own, 1), rows)]
    rotation = jax.random.randint(jax.random.fold_in(own, 2), (rows, 1), 0, top)
    return jnp.take_along_axis(grid, (jnp.arange(top)[None, :] + rotation) % top, axis=1)


def load_shares(number_of, total, reach, lean, full):
    loads = [(1 << 20) // math.isqrt(standing ** lean) + 1 for standing in range(1, number_of + 1)]
    largest = reach if full else min(reach, max(-(-total // number_of), total * loads[0] // sum(loads)))
    least = 1 if total - largest >= number_of - 1 else 0
    counts, rest = [largest] + [least] * (number_of - 1), total - largest - least * (number_of - 1)
    while rest > 0:
        movable = [i for i in range(1, number_of) if counts[i] < largest] or [i for i in range(1, number_of) if counts[i] < reach]
        pool, left = sum([loads[i] for i in movable]), rest
        for i in movable:
            addition = min(reach - counts[i], max(1, left * loads[i] // pool), rest)
            counts[i] = counts[i] + addition
            rest = rest - addition
    return np.array(counts)


def normal_values(stream_key, extent, width, limit, cuts=(), held_as=jnp.bfloat16):
    entries = width * jax.random.normal(stream_key, extent, jnp.float32)
    if cuts:
        entries = entries * level_of(stream_key, extent, cuts, -0.22, 0.18)
    return jnp.clip(entries, -limit, limit).astype(held_as)


def setup_inputs(seed: int = 0, part: int = 0) -> dict:
    key_list = jax.random.split(jax.random.key(seed), 10)
    part_splits = jax.random.split(jax.random.fold_in(key_list[9], part), 10)
    hidden_act = normal_values(part_splits[0], (STEPS, ROWS, TOPK, FW), 1.0, 6.0, ((1, 16),))
    routes_keys = jax.random.split(jax.random.fold_in(part_splits[1], 1), STEPS * ROWS // ROWS_DEV)
    routes_turns = jax.random.permutation(jax.random.fold_in(part_splits[1], 3), STEPS * ROWS // ROWS_DEV)
    routes = jax.vmap(lambda own, number: deal_out(jax.random.fold_in(part_splits[1], 2), own, number, ROWS_DEV, E, TOPK, CAP, 2))(routes_keys, routes_turns).reshape((STEPS, ROWS, TOPK))
    gates = jnp.clip(jnp.exp(math.log(1.0) - 2.3025851 * jax.random.uniform(part_splits[2], (STEPS, ROWS, TOPK), jnp.float32) ** level_of(part_splits[2], (STEPS, ROWS, TOPK), ((1, 16),), -0.2, 0.2)), 0.1, 1.0)
    down_codes = draw_down_codes(jax.random.fold_in(key_list[9], 71), part)
    down_scales = jnp.clip(jnp.exp(math.log(0.05) - 1.609438 * jax.random.uniform(key_list[4], (E, FW // BLK, D // BLK), jnp.float32) ** level_of(key_list[4], (E, FW // BLK, D // BLK), ((0, 16),), -0.2, 0.2)), 0.01, 0.05)
    changed = draw_changed(jax.random.fold_in(jax.random.fold_in(key_list[9], part), 71), part)
    fresh_codes = draw_fresh_codes(jax.random.fold_in(jax.random.fold_in(key_list[9], part), 71), part)
    fresh_scales = jnp.clip(jnp.exp(math.log(0.05) - 1.609438 * jax.random.uniform(part_splits[7], (CHANGED, N_LEARNER, BPH), jnp.float32) ** level_of(part_splits[7], (CHANGED, N_LEARNER, BPH), ((2, 16),), -0.2, 0.2)), 0.01, 0.05)
    block_ids = jax.vmap(lambda own: jax.random.permutation(own, BPH))(jax.random.split(part_splits[8], CHANGED * N_LEARNER)).reshape((CHANGED, N_LEARNER, BPH)).astype(jnp.int32)
    return {"hidden_act": hidden_act, "routes": routes, "gates": gates, "down_codes": down_codes, "down_scales": down_scales, "changed": changed, "fresh_codes": fresh_codes, "fresh_scales": fresh_scales, "block_ids": block_ids}


def dequant(code_grid, scale_grid):
    rows_in, cols_in = code_grid.shape[-2], code_grid.shape[-1]
    lead = code_grid.shape[:-2]
    blocks = code_grid.astype(jnp.float32).reshape(lead + (rows_in // BLK, BLK, cols_in // BLK, BLK))
    scaled = blocks * scale_grid[..., :, None, :, None]
    return scaled.reshape(code_grid.shape).astype(jnp.bfloat16)


def assemble(codes_one, scales_one, order_one):
    values = (codes_one.astype(jnp.float32) * scales_one[..., None, None]).astype(jnp.bfloat16)
    halves = []
    for half_index in range(N_LEARNER):
        placed = jnp.zeros_like(values[half_index]).at[order_one[half_index]].set(values[half_index])
        assembled = placed.reshape(FW // BLK, D // (BLK * N_LEARNER), BLK, BLK)
        assembled = assembled.transpose(0, 2, 1, 3).reshape(FW, D // N_LEARNER)
        halves.append(assembled)
    return jnp.concatenate(halves, axis=1)


def expert_layer(activations, route_rows, gate_rows, weights):
    flat_act = activations.reshape(ROWS * TOPK, FW)
    flat_route = route_rows.reshape(-1)
    flat_gate = gate_rows.reshape(-1)
    row_of = jnp.arange(ROWS * TOPK, dtype=jnp.int32) // TOPK
    slot_count = N_EXPERT * N_LEARNER * CAP

    def per_expert(combined, expert_id):
        matches = flat_route == expert_id
        members = jnp.nonzero(matches, size=slot_count, fill_value=0)[0].astype(jnp.int32)
        is_live = jnp.arange(slot_count, dtype=jnp.int32) < jnp.sum(matches.astype(jnp.int32))
        product = jnp.dot(flat_act[members], weights[expert_id], preferred_element_type=jnp.float32)
        product = lax.optimization_barrier(product.astype(jnp.bfloat16)).astype(jnp.float32)
        weight_of = jnp.where(is_live, flat_gate[members], jnp.zeros_like(flat_gate[members]))
        combined = combined.at[row_of[members]].add(weight_of[:, None] * product)
        return combined, None

    start = jnp.zeros((ROWS, D), jnp.float32)
    combined, _ = lax.scan(per_expert, start, jnp.arange(E, dtype=jnp.int32))
    return combined.astype(jnp.bfloat16)


def reference(hidden_act, routes, gates, down_codes, down_scales, changed, fresh_codes, fresh_scales, block_ids):
    old_weights = dequant(down_codes, down_scales)
    new_blocks = jax.vmap(assemble)(fresh_codes, fresh_scales, block_ids)
    refreshed = old_weights.at[changed].set(new_blocks)
    outputs = []
    for step_index in range(STEPS):
        weights = old_weights if step_index == 0 else refreshed
        outputs.append(expert_layer(hidden_act[step_index], routes[step_index], gates[step_index], weights))
    return jnp.stack(outputs)
```

```python
import functools

import jax
import jax.numpy as jnp
import numpy as np
from jax import lax
from jax.experimental import pallas as pl
from jax.experimental.pallas import tpu as pltpu
from jax.sharding import PartitionSpec as P

BLK = 128
LANES = 128
PAD_ROWS = 16
VMEM_LIMIT = 56 * 1024 * 1024
F32 = jnp.float32
BF16 = jnp.bfloat16


def old_kernel(order_ref, scale_ref, act_ref, code_ref, keep_ref, send_ref, act_scratch, weight_scratch):
    tile = pl.program_id(0)
    groups, group_rows, width = act_ref.shape
    tile_cols = code_ref.shape[1]

    @pl.when(tile == 0)
    def _():
        for g in range(groups):
            act_scratch[g * group_rows : (g + 1) * group_rows, :] = act_ref[order_ref[g]]

    per_tile = tile_cols // BLK
    col_blocks = pl.num_programs(0) * per_tile
    for i in range(width // BLK):
        for j in range(per_tile):
            scale = scale_ref[i * col_blocks + tile * per_tile + j]
            block = code_ref[i * BLK : (i + 1) * BLK, j * BLK : (j + 1) * BLK]
            weight_scratch[i * BLK : (i + 1) * BLK, j * BLK : (j + 1) * BLK] = (
                block.astype(F32) * scale
            ).astype(BF16)
    product = jnp.dot(act_scratch[...], weight_scratch[...], preferred_element_type=F32).astype(BF16)
    half = keep_ref.shape[0]
    keep_ref[...] = product[:half]
    send_ref[...] = product[half:]


def old_product(act, codes, scales, order):
    groups, group_rows, width = act.shape
    rows = groups * group_rows
    cols = codes.shape[1]
    tile_cols = 512
    half = rows // 2
    return pl.pallas_call(
        old_kernel,
        grid_spec=pltpu.PrefetchScalarGridSpec(
            num_scalar_prefetch=2,
            grid=(cols // tile_cols,),
            in_specs=[
                pl.BlockSpec((groups, group_rows, width), lambda t, *_: (0, 0, 0)),
                pl.BlockSpec((width, tile_cols), lambda t, *_: (0, t)),
            ],
            out_specs=[
                pl.BlockSpec((half, tile_cols), lambda t, *_: (0, t)),
                pl.BlockSpec((half, tile_cols), lambda t, *_: (0, t)),
            ],
            scratch_shapes=[pltpu.VMEM((rows, width), BF16), pltpu.VMEM((width, tile_cols), BF16)],
        ),
        out_shape=[jax.ShapeDtypeStruct((half, cols), BF16)] * 2,
        compiler_params=pltpu.CompilerParams(vmem_limit_bytes=VMEM_LIMIT),
        cost_estimate=pl.CostEstimate(
            flops=2 * rows * width * cols, bytes_accessed=2 * width * cols + 2 * rows * cols, transcendentals=0
        ),
        name="old_product",
    )(order, scales.reshape(-1), act, codes)


def fresh_kernel(
    n_pieces, experts, row_count, top_count,
    pos_ref, start_ref, slot_ref, index_ref, scale_ref,
    *refs,
):
    pieces = refs[:n_pieces]
    code_hbm, keep_ref, send_ref, act_buf, dense, code_buf, act_sem, code_sem = refs[n_pieces:]
    chunk = pl.program_id(0)
    groups, piece_rows, width = act_buf.shape
    row_blocks = width // BLK
    routed = row_count * top_count

    @pl.when(chunk == 0)
    def _():
        for i in range(n_pieces):
            pltpu.make_async_copy(pieces[i], act_buf.at[pos_ref[i]], act_sem.at[i]).start()
        pltpu.make_async_copy(code_hbm, code_buf, code_sem).start()
        for i in range(n_pieces):
            pltpu.make_async_copy(pieces[i], act_buf.at[pos_ref[i]], act_sem.at[i]).wait()
        row = lax.broadcasted_iota(jnp.int32, (experts * row_count, routed), 0)
        col = lax.broadcasted_iota(jnp.int32, (experts * row_count, routed), 1)
        same_row = row % row_count == col // top_count
        expert = (row // row_count).astype(F32)

        def expand(g, carry):
            route = act_buf[g, routed : routed + PAD_ROWS, 0:routed].astype(F32)[0:1, :]
            pick = jnp.where(same_row & (expert == route), 1.0, 0.0).astype(BF16)
            spread = jnp.dot(pick, act_buf[g, 0:routed, :], preferred_element_type=F32).astype(BF16)
            at = pl.ds(pl.multiple_of(g * row_count, row_count), row_count)
            for e in range(experts):
                for b in range(row_blocks):
                    dense[e * row_blocks + b, at, :] = spread[
                        e * row_count : (e + 1) * row_count, b * BLK : (b + 1) * BLK
                    ]
            return carry

        lax.fori_loop(0, groups, expand, 0)
        pltpu.make_async_copy(code_hbm, code_buf, code_sem).wait()

    per_chunk = keep_ref.shape[1] // BLK
    half = keep_ref.shape[0]
    rows = 2 * half
    for j in range(per_chunk):
        column = chunk * per_chunk + j
        first = start_ref[column]
        last = start_ref[column + 1]

        def pair(t, total):
            one = first + 2 * t
            two = jnp.minimum(one + 1, last - 1)
            scale_two = jnp.where(one + 1 < last, scale_ref[two], 0.0)
            block_one = (code_buf[slot_ref[one]].astype(F32) * scale_ref[one]).astype(BF16)
            block_two = (code_buf[slot_ref[two]].astype(F32) * scale_two).astype(BF16)
            left = jnp.concatenate([dense[index_ref[one]], dense[index_ref[two]]], axis=1)
            right = jnp.concatenate([block_one, block_two], axis=0)
            return total + jnp.dot(left, right, preferred_element_type=F32)

        total = lax.fori_loop(0, (last - first + 1) // 2, pair, jnp.zeros((rows, BLK), F32))
        total = total.astype(BF16)
        keep_ref[:, j * BLK : (j + 1) * BLK] = total[:half]
        send_ref[:, j * BLK : (j + 1) * BLK] = total[half:]


def fresh_product(pieces, pos, codes, plan, cols, experts, row_count, top_count):
    n_pieces = len(pieces)
    piece_rows, width = pieces[0].shape
    rows = n_pieces * row_count
    slots = codes.shape[0]
    chunk_cols = cols // 7
    half = rows // 2
    return pl.pallas_call(
        functools.partial(fresh_kernel, n_pieces, experts, row_count, top_count),
        grid_spec=pltpu.PrefetchScalarGridSpec(
            num_scalar_prefetch=5,
            grid=(cols // chunk_cols,),
            in_specs=[pl.BlockSpec(memory_space=pl.ANY)] * (n_pieces + 1),
            out_specs=[
                pl.BlockSpec((half, chunk_cols), lambda t, *_: (0, t)),
                pl.BlockSpec((half, chunk_cols), lambda t, *_: (0, t)),
            ],
            scratch_shapes=[
                pltpu.VMEM((n_pieces, piece_rows, width), BF16),
                pltpu.VMEM((experts * (width // BLK), rows, BLK), BF16),
                pltpu.VMEM(codes.shape, BF16),
                pltpu.SemaphoreType.DMA((n_pieces,)),
                pltpu.SemaphoreType.DMA,
            ],
        ),
        out_shape=[jax.ShapeDtypeStruct((half, cols), BF16)] * 2,
        compiler_params=pltpu.CompilerParams(vmem_limit_bytes=VMEM_LIMIT),
        cost_estimate=pl.CostEstimate(
            flops=2 * rows * BLK * BLK * slots,
            bytes_accessed=2 * slots * BLK * BLK + 2 * rows * cols + 2 * rows * width * 8,
            transcendentals=0,
        ),
        name="fresh_product",
    )(pos, *plan, *pieces, codes)


def fresh_plan(own_ids, own_scales, changed, col_blocks, row_blocks):
    slots_each = own_ids.shape[1]
    ids = own_ids.reshape(-1)
    count = ids.shape[0]
    column = ids % col_blocks
    index = jnp.repeat(changed, slots_each) * row_blocks + ids // col_blocks
    number = jnp.arange(count, dtype=jnp.int32)
    key = column * count + number
    rank = jnp.sum((key[None, :] < key[:, None]).astype(jnp.int32), axis=1)
    hit = rank[None, :] == number[:, None]
    slot = jnp.sum(jnp.where(hit, number[None, :], 0), axis=1)
    sorted_index = jnp.sum(jnp.where(hit, index[None, :], 0), axis=1)
    sorted_scale = jnp.sum(jnp.where(hit, own_scales.reshape(-1)[None, :], 0.0), axis=1)
    bounds = jnp.arange(col_blocks + 1, dtype=jnp.int32)
    start = jnp.sum((column[None, :] < bounds[:, None]).astype(jnp.int32), axis=1)
    return start, slot, sorted_index, sorted_scale


def add(*terms):
    total = terms[0].astype(F32)
    for term in terms[1:]:
        total = total + term.astype(F32)
    return total.astype(BF16)


class ChipGrid:
    SIZE = 16
    CYCLE = [(0, 0), (1, 0), (2, 0), (3, 0), (3, 1), (2, 1), (1, 1), (0, 1)]

    def __init__(self):
        cycle = self.CYCLE
        n = len(cycle)
        at = {chip: i for i, chip in enumerate(cycle)}
        number = lambda z, y, c: (z * 2 + y) * 2 + c
        self.forward, self.backward = [], []
        self.piece_rank = np.zeros((self.SIZE, self.SIZE), np.int32)
        self.rank_source = np.zeros((self.SIZE, self.SIZE), np.int32)
        for z in range(4):
            for y in range(2):
                for c in range(2):
                    me, i = number(z, y, c), at[(z, y)]
                    self.forward.append((me, number(*cycle[(i + 1) % n], c)))
                    self.backward.append((me, number(*cycle[(i - 1) % n], c)))
                    hops = [0, -1, 1, -2, 2, -3, 3, -4]
                    for dc in range(2):
                        for k, hop in enumerate(hops):
                            sz, sy = cycle[(i + hop) % n]
                            self.piece_rank[me, dc * 8 + k] = self.rank(sz ^ z, sy ^ y, dc)
                    for dz in range(4):
                        for dy in range(2):
                            for dc in range(2):
                                self.rank_source[me, self.rank(dz, dy, dc)] = number(z ^ dz, y ^ dy, c ^ dc)

    @staticmethod
    def rank(dz, dy, dc):
        return dc * 8 + dy * 4 + dz

    def partner(self, x, dz, dy, dc):
        delta = (dz * 2 + dy) * 2 + dc
        return lax.ppermute(x, "expert", [(i, i ^ delta) for i in range(self.SIZE)])

    def gather(self, x):
        ahead = behind = x
        got = [x]
        for step in range(4):
            ahead = lax.ppermute(ahead, "expert", self.forward)
            got.append(ahead)
            if step < 3:
                behind = lax.ppermute(behind, "expert", self.backward)
                got.append(behind)
        return got + [self.partner(piece, 0, 0, 1) for piece in got]

    def reduce(self, keep, send, rows):
        got = self.partner(send, 0, 0, 1)
        per_y = 4 * rows
        far = add(keep[per_y:], got[per_y:])
        far = self.partner(far, 0, 1, 0)
        near = [
            add(keep[k * rows : (k + 1) * rows], got[k * rows : (k + 1) * rows], far[k * rows : (k + 1) * rows])
            for k in range(4)
        ]
        moved = [self.partner(near[dz], dz, 0, 0) for dz in (1, 2, 3)]
        return add(near[0], *moved)


def body(
    hidden_act,
    routes,
    gates,
    down_codes,
    down_scales,
    changed,
    fresh_codes,
    fresh_scales,
    block_ids,
):
    experts = lax.axis_size("expert")
    learners = lax.axis_size("learner")
    own = lax.axis_index("expert")
    own_half = lax.axis_index("learner")
    step_count, row_count, top_count, width = hidden_act.shape
    cols = down_codes.shape[2]
    routed = row_count * top_count
    row_blocks, col_blocks = width // BLK, cols // BLK
    slots_each = fresh_codes.shape[2]
    some_unchanged = changed.shape[0] < experts

    gated = (hidden_act.astype(F32) * gates[..., None]).astype(BF16).reshape(step_count, routed, width)
    flat_routes = routes.reshape(step_count, routed)
    row = jnp.arange(experts * row_count, dtype=jnp.int32)
    entry = jnp.arange(routed, dtype=jnp.int32)

    def spread(step):
        pick = (row[:, None] // row_count == flat_routes[step][None, :]) & (
            row[:, None] % row_count == entry[None, :] // top_count
        )
        out = jnp.dot(pick.astype(BF16), gated[step], preferred_element_type=F32)
        return out.astype(BF16).reshape(experts, row_count, width)

    def with_routes(step):
        tail = jnp.zeros((PAD_ROWS, width), BF16).at[0, :routed].set(flat_routes[step].astype(BF16))
        return jnp.concatenate([gated[step], tail], axis=0)

    own_ids = lax.dynamic_slice_in_dim(block_ids[:, own_half], own * slots_each, slots_each, axis=1)
    plan = fresh_plan(own_ids, fresh_scales[:, 0], changed, col_blocks, row_blocks)
    codes = fresh_codes.reshape((-1, BLK, BLK))
    scales = down_scales[0]

    if experts == ChipGrid.SIZE and learners == 1 and not some_unchanged:
        grid = ChipGrid()
        order = jnp.asarray(grid.rank_source)[own]
        pos = jnp.asarray(grid.piece_rank)[own]
        dense_old = lax.all_to_all(spread(0), "expert", split_axis=0, concat_axis=0, tiled=True)
        pieces = {step: grid.gather(with_routes(step)) for step in range(1, step_count)}
        results = [grid.reduce(*old_product(dense_old, down_codes[0], scales, order), row_count)]
        for step in range(1, step_count):
            halves = fresh_product(pieces[step], pos, codes, plan, cols, experts, row_count, top_count)
            results.append(grid.reduce(*halves, row_count))
        return jnp.stack(results)

    group = experts * learners
    straight = jnp.arange(group, dtype=jnp.int32)

    def combine(keep, send):
        part = jnp.concatenate([keep, send], axis=0)
        summed = lax.psum_scatter(part, "expert", scatter_dimension=0, tiled=True)
        return lax.all_to_all(summed, "learner", split_axis=0, concat_axis=1, tiled=True)

    def old_part(step):
        dense = lax.all_to_all(spread(step), "expert", split_axis=0, concat_axis=0, tiled=True)
        if step > 0:
            dense = jnp.where(jnp.any(changed == own), jnp.zeros_like(dense), dense)
        dense = lax.all_gather(dense, "learner", axis=1, tiled=False)
        dense = dense.reshape(group, row_count, width)
        return old_product(dense, down_codes[0], scales, straight)

    results = [combine(*old_part(0))]
    at_once = 16
    for step in range(1, step_count):
        everyone = lax.all_gather(with_routes(step), ("expert", "learner"), axis=0)
        keep_rows, send_rows = [], []
        for first in range(0, group, at_once):
            pieces = [everyone[first + i] for i in range(at_once)]
            keep, send = fresh_product(
                pieces, straight[:at_once], codes, plan, cols, experts, row_count, top_count
            )
            keep_rows.append(jnp.concatenate([keep, send], axis=0))
        total = jnp.concatenate(keep_rows, axis=0)
        if some_unchanged:
            total = add(total, jnp.concatenate(old_part(step), axis=0))
        results.append(combine(total[: total.shape[0] // 2], total[total.shape[0] // 2 :]))
    return jnp.stack(results)


def solution(mesh):
    in_specs = (
        P(None, ("groups", "expert", "learner"), None, None),
        P(None, ("groups", "expert", "learner"), None),
        P(None, ("groups", "expert", "learner"), None),
        P("expert", None, "learner"),
        P("expert", None, "learner"),
        P("groups"),
        P("groups", "learner", "expert", None, None),
        P("groups", "learner", "expert"),
        P("groups", None, None),
    )
    out_specs = P(None, ("groups", "expert", "learner"), None)
    return jax.shard_map(body, mesh=mesh, in_specs=in_specs, out_specs=out_specs, check_vma=False)
```

```python
import functools

import jax
import jax.numpy as jnp
import numpy as np
from jax import lax
from jax.experimental import pallas as pl
from jax.experimental.pallas import tpu as pltpu
from jax.sharding import PartitionSpec as P

BLK = 128
LANES = 128
PAD_ROWS = 16
PAIRS = 16
SPARE_VMEM = 3 * 1024 * 1024
F32 = jnp.float32
BF16 = jnp.bfloat16


def in_vmem(x):
    return pltpu.with_memory_space_constraint(x, pltpu.VMEM)


def old_kernel(order_ref, scale_ref, act_ref, code_hbm, keep_ref, send_ref, act_scratch, code_buf, code_sem):
    groups, group_rows, width = act_ref.shape
    chunks, _, chunk_cols = code_buf.shape

    def arrival(c):
        columns = pl.ds(c * chunk_cols, chunk_cols)
        return pltpu.make_async_copy(code_hbm.at[:, columns], code_buf.at[c], code_sem.at[c])

    for c in range(chunks):
        arrival(c).start()
    for g in range(groups):
        act_scratch[g * group_rows : (g + 1) * group_rows, :] = act_ref[order_ref[g]]
    act = act_scratch[...]
    half = act.shape[0] // 2
    per_chunk = chunk_cols // BLK
    for c in range(chunks):
        arrival(c).wait()
        for t in range(0, per_chunk, 2):
            rows = []
            for i in range(width // BLK):
                pair = []
                for j in range(t, t + 2):
                    block = code_buf[c, i * BLK : (i + 1) * BLK, j * BLK : (j + 1) * BLK]
                    scale = scale_ref[i * chunks * per_chunk + c * per_chunk + j]
                    pair.append((block.astype(F32) * scale).astype(BF16))
                rows.append(jnp.concatenate(pair, axis=1))
            weight = jnp.concatenate(rows, axis=0)
            product = jnp.dot(act, weight, preferred_element_type=F32).astype(BF16)
            at = slice(c * chunk_cols + t * BLK, c * chunk_cols + (t + 2) * BLK)
            keep_ref[:, at] = product[:half]
            send_ref[:, at] = product[half:]


def halves_of(rows, part_blocks):
    shapes = []
    for blocks in part_blocks:
        shapes += [pltpu.VMEM((rows // 2, blocks * BLK), BF16)] * 2
    return shapes


def old_product(act, codes, scales, order):
    groups, group_rows, width = act.shape
    rows, cols = groups * group_rows, codes.shape[1]
    chunks = cols // (14 * BLK)
    whole = pl.BlockSpec(memory_space=pltpu.VMEM)
    return pl.pallas_call(
        old_kernel,
        grid_spec=pltpu.PrefetchScalarGridSpec(
            num_scalar_prefetch=2,
            grid=(),
            in_specs=[whole, pl.BlockSpec(memory_space=pl.ANY)],
            out_specs=[whole] * 2,
            scratch_shapes=[
                pltpu.VMEM((rows, width), BF16),
                pltpu.VMEM((chunks, width, cols // chunks), BF16),
                pltpu.SemaphoreType.DMA((chunks,)),
            ],
        ),
        out_shape=halves_of(rows, (cols // BLK,)),
        compiler_params=pltpu.CompilerParams(vmem_limit_bytes=2 * (rows + cols) * width + SPARE_VMEM),
        cost_estimate=pl.CostEstimate(
            flops=2 * rows * width * cols, bytes_accessed=2 * width * cols + 2 * rows * cols, transcendentals=0
        ),
        name="old_product",
    )(order, scales.reshape(-1), in_vmem(act), pltpu.with_memory_space_constraint(codes, pltpu.HBM))


def fresh_kernel(
    n_pieces, experts, row_count, top_count, part_blocks,
    pos_ref, steps_ref, column_ref, slot_ref, index_ref, scale_ref,
    *refs,
):
    pieces, code_ref = refs[:n_pieces], refs[n_pieces]
    outs, dense, total = refs[n_pieces + 1 : -2], refs[-2], refs[-1]
    width = pieces[0].shape[1]
    row_blocks = width // BLK
    routed = row_count * top_count
    slots = code_ref.shape[0]
    half = dense.shape[1] // 2

    row = lax.broadcasted_iota(jnp.int32, (experts * row_count, routed), 0)
    col = lax.broadcasted_iota(jnp.int32, (experts * row_count, routed), 1)
    same_row = row % row_count == col // top_count
    expert = (row // row_count).astype(F32)
    for i in range(n_pieces):
        route = pieces[i][routed : routed + PAD_ROWS, 0:routed].astype(F32)[0:1, :]
        pick = jnp.where(same_row & (expert == route), 1.0, 0.0).astype(BF16)
        spread = jnp.dot(pick, pieces[i][0:routed, :], preferred_element_type=F32).astype(BF16)
        at = pl.ds(pl.multiple_of(pos_ref[i] * row_count, row_count), row_count)
        for e in range(experts):
            for b in range(row_blocks):
                dense[e * row_blocks + b, at, :] = spread[
                    e * row_count : (e + 1) * row_count, b * BLK : (b + 1) * BLK
                ]

    def clear(j, carry):
        total[j] = jnp.zeros(total.shape[1:], F32)
        return carry

    def some_pairs(t, carry):
        products = []
        for u in range(PAIRS):
            number = t * PAIRS + u
            left, right = [], []
            for q in range(2):
                slot = slot_ref[2 * number + q]
                block = code_ref[jnp.minimum(slot, slots - 1)]
                right.append((block.astype(F32) * scale_ref[slot]).astype(BF16))
                left.append(dense[index_ref[slot]])
            left, right = jnp.concatenate(left, axis=1), jnp.concatenate(right, axis=0)
            products.append(jnp.dot(left, right, preferred_element_type=F32))
        for u in range(PAIRS):
            total[column_ref[t * PAIRS + u]] += products[u]
        return carry

    lax.fori_loop(0, total.shape[0], clear, 0)
    lax.fori_loop(0, steps_ref[0], some_pairs, 0)
    first = 0
    for part, blocks in enumerate(part_blocks):
        for j in range(blocks):
            done = total[first + j].astype(BF16)
            outs[2 * part][:, j * BLK : (j + 1) * BLK] = done[:half]
            outs[2 * part + 1][:, j * BLK : (j + 1) * BLK] = done[half:]
        first += blocks


def fresh_product(pieces, pos, codes, plan, part_blocks, experts, row_count, top_count):
    n_pieces = len(pieces)
    rows, cols = n_pieces * row_count, sum(part_blocks) * BLK
    width = pieces[0].shape[1]
    slots = codes.shape[0]
    whole = pl.BlockSpec(memory_space=pltpu.VMEM)
    outs = pl.pallas_call(
        functools.partial(fresh_kernel, n_pieces, experts, row_count, top_count, part_blocks),
        grid_spec=pltpu.PrefetchScalarGridSpec(
            num_scalar_prefetch=6,
            grid=(),
            in_specs=[whole] * (n_pieces + 1),
            out_specs=[whole] * (2 * len(part_blocks)),
            scratch_shapes=[
                pltpu.VMEM((experts * (width // BLK), rows, BLK), BF16),
                pltpu.VMEM((sum(part_blocks), rows, BLK), F32),
            ],
        ),
        out_shape=halves_of(rows, part_blocks),
        compiler_params=pltpu.CompilerParams(
            vmem_limit_bytes=2 * experts * width * rows + 4 * rows * cols + SPARE_VMEM
        ),
        cost_estimate=pl.CostEstimate(
            flops=2 * rows * BLK * BLK * slots, bytes_accessed=2 * slots * BLK * BLK + 2 * rows * cols, transcendentals=0
        ),
        name="fresh_product",
    )(pos, *plan, *[in_vmem(piece) for piece in pieces], in_vmem(codes))
    return [outs[2 * i : 2 * i + 2] for i in range(len(part_blocks))]


def fresh_plan(own_ids, own_scales, changed, col_blocks, row_blocks):
    slots_each = own_ids.shape[1]
    ids = own_ids.reshape(-1)
    count = ids.shape[0]
    column = ids % col_blocks
    index = jnp.repeat(changed, slots_each) * row_blocks + ids // col_blocks
    number = jnp.arange(count, dtype=jnp.int32)
    columns = jnp.arange(col_blocks, dtype=jnp.int32)
    most = -(-(count // 2 + (col_blocks + 1) // 2) // PAIRS) * PAIRS
    pairs = (jnp.sum((column[None, :] == columns[:, None]).astype(jnp.int32), axis=1) + 1) // 2
    before = jnp.sum(jnp.where(columns[None, :] < column[:, None], pairs[None, :], 0), axis=1)
    earlier = (column[None, :] == column[:, None]) & (number[None, :] < number[:, None])
    place = 2 * before + jnp.sum(earlier.astype(jnp.int32), axis=1)
    places = jnp.arange(2 * most, dtype=jnp.int32)
    slot = count - jnp.sum(jnp.where(place[None, :] == places[:, None], count - number[None, :], 0), axis=1)
    ends = jnp.sum(jnp.where(columns[None, :] <= columns[:, None], pairs[None, :], 0), axis=1)
    pair_column = jnp.sum((ends[None, :] <= places[:most, None]).astype(jnp.int32), axis=1)
    pair_column = jnp.minimum(pair_column, col_blocks - 1)
    steps = (ends[-1:] + PAIRS - 1) // PAIRS
    return steps, pair_column, slot, jnp.pad(index, (0, 1)), jnp.pad(own_scales.reshape(-1), (0, 1))


def add(*terms):
    total = terms[0].astype(F32)
    for term in terms[1:]:
        total = total + term.astype(F32)
    return total.astype(BF16)


class ChipGrid:
    SIZE = 16
    CYCLE = [(0, 0), (1, 0), (2, 0), (3, 0), (3, 1), (2, 1), (1, 1), (0, 1)]

    def __init__(self):
        cycle = self.CYCLE
        n = len(cycle)
        at = {chip: i for i, chip in enumerate(cycle)}
        number = lambda z, y, c: (z * 2 + y) * 2 + c
        self.forward, self.backward = [], []
        self.piece_rank = np.zeros((self.SIZE, self.SIZE), np.int32)
        self.rank_source = np.zeros((self.SIZE, self.SIZE), np.int32)
        for z in range(4):
            for y in range(2):
                for c in range(2):
                    me, i = number(z, y, c), at[(z, y)]
                    self.forward.append((me, number(*cycle[(i + 1) % n], c)))
                    self.backward.append((me, number(*cycle[(i - 1) % n], c)))
                    hops = [0, -1, 1, -2, 2, -3, 3, -4]
                    for dc in range(2):
                        for k, hop in enumerate(hops):
                            sz, sy = cycle[(i + hop) % n]
                            self.piece_rank[me, dc * 8 + k] = self.rank(sz ^ z, sy ^ y, dc)
                    for dz in range(4):
                        for dy in range(2):
                            for dc in range(2):
                                self.rank_source[me, self.rank(dz, dy, dc)] = number(z ^ dz, y ^ dy, c ^ dc)

    @staticmethod
    def rank(dz, dy, dc):
        return dc * 8 + dy * 4 + (dz % 2) * 2 + dz // 2

    def partner(self, x, dz, dy, dc):
        delta = (dz * 2 + dy) * 2 + dc
        return lax.ppermute(x, "expert", [(i, i ^ delta) for i in range(self.SIZE)])

    def ahead(self, x):
        return lax.ppermute(x, "expert", self.forward)

    def behind(self, x):
        return lax.ppermute(x, "expert", self.backward)

    def other_core(self, x):
        return self.partner(x, 0, 0, 1)

    def other_y(self, x):
        return self.partner(x, 0, 1, 0)

    def near_z(self, x):
        return self.partner(x, 1, 0, 0)

    def far_z(self, x):
        return self.partner(x, 2, 0, 0)


def add_rows(first, last, *terms):
    return add(*[term[first:last] for term in terms])


def body(
    hidden_act,
    routes,
    gates,
    down_codes,
    down_scales,
    changed,
    fresh_codes,
    fresh_scales,
    block_ids,
):
    experts = lax.axis_size("expert")
    learners = lax.axis_size("learner")
    own = lax.axis_index("expert")
    own_half = lax.axis_index("learner")
    step_count, row_count, top_count, width = hidden_act.shape
    cols = down_codes.shape[2]
    routed = row_count * top_count
    row_blocks, col_blocks = width // BLK, cols // BLK
    slots_each = fresh_codes.shape[2]
    some_unchanged = changed.shape[0] < experts

    gated = (hidden_act.astype(F32) * gates[..., None]).astype(BF16).reshape(step_count, routed, width)
    flat_routes = routes.reshape(step_count, routed)
    row = jnp.arange(experts * row_count, dtype=jnp.int32)
    entry = jnp.arange(routed, dtype=jnp.int32)

    def spread(step):
        pick = (row[:, None] // row_count == flat_routes[step][None, :]) & (
            row[:, None] % row_count == entry[None, :] // top_count
        )
        out = jnp.dot(pick.astype(BF16), gated[step], preferred_element_type=F32)
        return out.astype(BF16).reshape(experts, row_count, width)

    def with_routes(step):
        tail = jnp.zeros((PAD_ROWS, width), BF16).at[0, :routed].set(flat_routes[step].astype(BF16))
        return jnp.concatenate([gated[step], tail], axis=0)

    codes = fresh_codes.reshape((-1, BLK, BLK))
    scales = down_scales[0]

    part_blocks = (2 * (col_blocks // 4), col_blocks - 2 * (col_blocks // 4))

    def fresh_order(changed, block_ids):
        first = own * slots_each
        own_ids = lax.dynamic_slice_in_dim(block_ids[:, own_half], first, slots_each, axis=1)
        return fresh_plan(own_ids, fresh_scales[:, 0], changed, col_blocks, row_blocks)

    def old(act, order):
        return old_product(act, down_codes[0], scales, order)

    def fresh(pieces, pos, plan):
        return fresh_product(pieces, pos, codes, plan, part_blocks, experts, row_count, top_count)

    if experts == ChipGrid.SIZE and learners == 1 and not some_unchanged and step_count == 2:
        grid = ChipGrid()
        together = lax.optimization_barrier
        order = jnp.asarray(grid.rank_source)[own]
        pos = jnp.asarray(grid.piece_rank)[own]
        unit = row_count

        x = with_routes(1)
        f1, b1 = grid.ahead(x), grid.behind(x)
        act_old = lax.all_to_all(spread(0), "expert", split_axis=0, concat_axis=0, tiled=True)
        f1, b1, order, pos, changed, block_ids = together((f1, b1, order, pos, changed, block_ids))

        f2, b2 = grid.ahead(f1), grid.behind(b1)
        cores = [grid.other_core(piece) for piece in (x, f1, b1)]
        plan = fresh_order(changed, block_ids)
        f2, b2, cores, act_old, plan = together((f2, b2, cores, act_old, plan))

        f3, b3 = grid.ahead(f2), grid.behind(b2)
        keep_old, send_old = old(act_old, order)
        f3, b3, keep_old, send_old = together((f3, b3, keep_old, send_old))

        f4 = grid.ahead(f3)
        got_old = grid.other_core(send_old)
        cores += [grid.other_core(piece) for piece in (f2, b2, f3, b3)]
        far_old = add_rows(4 * unit, 8 * unit, keep_old, got_old)
        f4, cores, far_old = together((f4, cores, far_old))

        cut = 2 * (col_blocks // 3) * BLK
        first_old = grid.other_y(far_old[:, :cut])
        pieces = [x, f1, b1, f2, b2, f3, b3, f4] + cores + [grid.other_core(f4)]
        (keep_c, send_c), (keep_d, send_d) = fresh(pieces, pos, plan)
        first_old, send_c, send_d = together((first_old, send_c, send_d))

        rest_old = grid.other_y(far_old[:, cut:])
        got_c, got_d = grid.other_core(send_c), grid.other_core(send_d)
        far_c = add_rows(4 * unit, 8 * unit, keep_c, got_c)
        far_d = add_rows(4 * unit, 8 * unit, keep_d, got_d)
        rest_old, far_c, far_d = together((rest_old, far_c, far_d))

        old_terms = [keep_old, got_old, jnp.concatenate([first_old, rest_old], axis=1)]
        far_c = grid.other_y(far_c)
        near_old = grid.near_z(add_rows(2 * unit, 4 * unit, *old_terms))
        far_c, near_old, far_d = together((far_c, near_old, far_d))

        old_terms = [term[: 2 * unit] for term in old_terms] + [near_old]
        c_terms = [keep_c, got_c, far_c]
        far_d = grid.other_y(far_d)
        near_c = grid.near_z(add_rows(2 * unit, 4 * unit, *c_terms))
        end_old = grid.far_z(add_rows(unit, 2 * unit, *old_terms))
        far_d, near_c, end_old = together((far_d, near_c, end_old))

        c_terms = [term[: 2 * unit] for term in c_terms] + [near_c]
        d_terms = [keep_d, got_d, far_d]
        near_d = grid.near_z(add_rows(2 * unit, 4 * unit, *d_terms))
        end_c = grid.far_z(add_rows(unit, 2 * unit, *c_terms))
        near_d, end_c = together((near_d, end_c))

        d_terms = [term[: 2 * unit] for term in d_terms] + [near_d]
        end_d = grid.far_z(add_rows(unit, 2 * unit, *d_terms))
        out_old = add_rows(0, unit, *old_terms, end_old)
        out_c = add_rows(0, unit, *c_terms, end_c)
        out_d = add_rows(0, unit, *d_terms, end_d)
        return jnp.stack([out_old, jnp.concatenate([out_c, out_d], axis=1)])

    group = experts * learners
    straight = jnp.arange(group, dtype=jnp.int32)

    def joined(halves):
        return jnp.concatenate([jnp.concatenate(half, axis=0) for half in halves], axis=1)

    def combine(part):
        summed = lax.psum_scatter(part, "expert", scatter_dimension=0, tiled=True)
        return lax.all_to_all(summed, "learner", split_axis=0, concat_axis=1, tiled=True)

    def old_part(step):
        dense = lax.all_to_all(spread(step), "expert", split_axis=0, concat_axis=0, tiled=True)
        if step > 0:
            dense = jnp.where(jnp.any(changed == own), jnp.zeros_like(dense), dense)
        dense = lax.all_gather(dense, "learner", axis=1, tiled=False)
        dense = dense.reshape(group, row_count, width)
        chunks = []
        for first in range(0, group, at_once):
            act = dense[first : first + at_once]
            chunks.append(joined([old(act, straight[:at_once])]))
        return jnp.concatenate(chunks, axis=0)

    def fresh_part(step):
        everyone = lax.all_gather(with_routes(step), ("expert", "learner"), axis=0)
        chunks = []
        for first in range(0, group, at_once):
            pieces = [everyone[first + i] for i in range(at_once)]
            chunks.append(joined(fresh(pieces, straight[:at_once], plan)))
        return jnp.concatenate(chunks, axis=0)

    at_once = min(group, 16)
    plan = fresh_order(changed, block_ids)
    results = [combine(old_part(0))]
    for step in range(1, step_count):
        total = fresh_part(step)
        if some_unchanged:
            total = add(total, old_part(step))
        results.append(combine(total))
    return jnp.stack(results)


def solution(mesh):
    in_specs = (
        P(None, ("groups", "expert", "learner"), None, None),
        P(None, ("groups", "expert", "learner"), None),
        P(None, ("groups", "expert", "learner"), None),
        P("expert", None, "learner"),
        P("expert", None, "learner"),
        P("groups"),
        P("groups", "learner", "expert", None, None),
        P("groups", "learner", "expert"),
        P("groups", None, None),
    )
    out_specs = P(None, ("groups", "expert", "learner"), None)
    return jax.shard_map(body, mesh=mesh, in_specs=in_specs, out_specs=out_specs, check_vma=False)
```

```python
import functools

import jax
import jax.numpy as jnp
import numpy as np
from jax import lax
from jax.experimental import pallas as pl
from jax.experimental.pallas import tpu as pltpu
from jax.sharding import PartitionSpec as P

BLK = 128
LANES = 128
PAD_ROWS = 16
PAIRS = 16
SPARE_VMEM = 3 * 1024 * 1024
F32 = jnp.float32
BF16 = jnp.bfloat16


def in_vmem(x):
    return pltpu.with_memory_space_constraint(x, pltpu.VMEM)


def old_kernel(order_ref, scale_ref, act_ref, code_hbm, keep_ref, send_ref, act_scratch, code_buf, code_sem):
    groups, group_rows, width = act_ref.shape
    chunks, _, chunk_cols = code_buf.shape

    def arrival(c):
        columns = pl.ds(c * chunk_cols, chunk_cols)
        return pltpu.make_async_copy(code_hbm.at[:, columns], code_buf.at[c], code_sem.at[c])

    for c in range(chunks):
        arrival(c).start()
    for g in range(groups):
        act_scratch[g * group_rows : (g + 1) * group_rows, :] = act_ref[order_ref[g]]
    act = act_scratch[...]
    half = act.shape[0] // 2
    per_chunk = chunk_cols // BLK
    for c in range(chunks):
        arrival(c).wait()
        for t in range(0, per_chunk, 2):
            rows = []
            for i in range(width // BLK):
                pair = []
                for j in range(t, t + 2):
                    block = code_buf[c, i * BLK : (i + 1) * BLK, j * BLK : (j + 1) * BLK]
                    scale = scale_ref[i * chunks * per_chunk + c * per_chunk + j]
                    pair.append((block.astype(F32) * scale).astype(BF16))
                rows.append(jnp.concatenate(pair, axis=1))
            weight = jnp.concatenate(rows, axis=0)
            product = jnp.dot(act, weight, preferred_element_type=F32).astype(BF16)
            at = slice(c * chunk_cols + t * BLK, c * chunk_cols + (t + 2) * BLK)
            keep_ref[:, at] = product[:half]
            send_ref[:, at] = product[half:]


def halves_of(rows, part_blocks):
    shapes = []
    for blocks in part_blocks:
        shapes += [pltpu.VMEM((rows // 2, blocks * BLK), BF16)] * 2
    return shapes


def old_product(act, codes, scales, order):
    groups, group_rows, width = act.shape
    rows, cols = groups * group_rows, codes.shape[1]
    chunks = cols // (14 * BLK)
    whole = pl.BlockSpec(memory_space=pltpu.VMEM)
    return pl.pallas_call(
        old_kernel,
        grid_spec=pltpu.PrefetchScalarGridSpec(
            num_scalar_prefetch=2,
            grid=(),
            in_specs=[whole, pl.BlockSpec(memory_space=pl.ANY)],
            out_specs=[whole] * 2,
            scratch_shapes=[
                pltpu.VMEM((rows, width), BF16),
                pltpu.VMEM((chunks, width, cols // chunks), BF16),
                pltpu.SemaphoreType.DMA((chunks,)),
            ],
        ),
        out_shape=halves_of(rows, (cols // BLK,)),
        compiler_params=pltpu.CompilerParams(vmem_limit_bytes=2 * (rows + cols) * width + SPARE_VMEM),
        cost_estimate=pl.CostEstimate(flops=0, bytes_accessed=0, transcendentals=0),
        name="old_product",
    )(order, scales.reshape(-1), in_vmem(act), pltpu.with_memory_space_constraint(codes, pltpu.HBM))


def fresh_kernel(
    n_pieces, experts, row_count, top_count, part_blocks,
    pos_ref, steps_ref, column_ref, slot_ref, index_ref, scale_ref,
    *refs,
):
    pieces, code_ref = refs[:n_pieces], refs[n_pieces]
    outs, dense, total = refs[n_pieces + 1 : -2], refs[-2], refs[-1]
    width = pieces[0].shape[1]
    row_blocks = width // BLK
    routed = row_count * top_count
    slots = code_ref.shape[0]
    half = dense.shape[1] // 2

    row = lax.broadcasted_iota(jnp.int32, (experts * row_count, routed), 0)
    col = lax.broadcasted_iota(jnp.int32, (experts * row_count, routed), 1)
    same_row = row % row_count == col // top_count
    expert = (row // row_count).astype(F32)
    for i in range(n_pieces):
        route = pieces[i][routed : routed + PAD_ROWS, 0:routed].astype(F32)[0:1, :]
        pick = jnp.where(same_row & (expert == route), 1.0, 0.0).astype(BF16)
        spread = jnp.dot(pick, pieces[i][0:routed, :], preferred_element_type=F32).astype(BF16)
        at = pl.ds(pl.multiple_of(pos_ref[i] * row_count, row_count), row_count)
        for e in range(experts):
            for b in range(row_blocks):
                dense[e * row_blocks + b, at, :] = spread[
                    e * row_count : (e + 1) * row_count, b * BLK : (b + 1) * BLK
                ]

    def clear(j, carry):
        total[j] = jnp.zeros(total.shape[1:], F32)
        return carry

    def some_pairs(t, carry):
        products = []
        for u in range(PAIRS):
            number = t * PAIRS + u
            left, right = [], []
            for q in range(2):
                slot = slot_ref[2 * number + q]
                block = code_ref[jnp.minimum(slot, slots - 1)]
                right.append((block.astype(F32) * scale_ref[slot]).astype(BF16))
                left.append(dense[index_ref[slot]])
            left, right = jnp.concatenate(left, axis=1), jnp.concatenate(right, axis=0)
            products.append(jnp.dot(left, right, preferred_element_type=F32))
        for u in range(PAIRS):
            total[column_ref[t * PAIRS + u]] += products[u]
        return carry

    lax.fori_loop(0, total.shape[0], clear, 0)
    lax.fori_loop(0, steps_ref[0], some_pairs, 0)
    first = 0
    for part, blocks in enumerate(part_blocks):
        for j in range(blocks):
            done = total[first + j].astype(BF16)
            outs[2 * part][:, j * BLK : (j + 1) * BLK] = done[:half]
            outs[2 * part + 1][:, j * BLK : (j + 1) * BLK] = done[half:]
        first += blocks


def fresh_product(pieces, pos, codes, plan, part_blocks, experts, row_count, top_count):
    n_pieces = len(pieces)
    rows, cols = n_pieces * row_count, sum(part_blocks) * BLK
    width = pieces[0].shape[1]
    slots = codes.shape[0]
    whole = pl.BlockSpec(memory_space=pltpu.VMEM)
    outs = pl.pallas_call(
        functools.partial(fresh_kernel, n_pieces, experts, row_count, top_count, part_blocks),
        grid_spec=pltpu.PrefetchScalarGridSpec(
            num_scalar_prefetch=6,
            grid=(),
            in_specs=[whole] * (n_pieces + 1),
            out_specs=[whole] * (2 * len(part_blocks)),
            scratch_shapes=[
                pltpu.VMEM((experts * (width // BLK), rows, BLK), BF16),
                pltpu.VMEM((sum(part_blocks), rows, BLK), F32),
            ],
        ),
        out_shape=halves_of(rows, part_blocks),
        compiler_params=pltpu.CompilerParams(
            vmem_limit_bytes=2 * experts * width * rows + 4 * rows * cols + SPARE_VMEM
        ),
        cost_estimate=pl.CostEstimate(flops=0, bytes_accessed=0, transcendentals=0),
        name="fresh_product",
    )(pos, *plan, *[in_vmem(piece) for piece in pieces], in_vmem(codes))
    return [outs[2 * i : 2 * i + 2] for i in range(len(part_blocks))]


def fresh_plan(own_ids, own_scales, changed, col_blocks, row_blocks):
    slots_each = own_ids.shape[1]
    ids = own_ids.reshape(-1)
    count = ids.shape[0]
    column = ids % col_blocks
    index = jnp.repeat(changed, slots_each) * row_blocks + ids // col_blocks
    number = jnp.arange(count, dtype=jnp.int32)
    columns = jnp.arange(col_blocks, dtype=jnp.int32)
    most = -(-(count // 2 + (col_blocks + 1) // 2) // PAIRS) * PAIRS
    pairs = (jnp.sum((column[None, :] == columns[:, None]).astype(jnp.int32), axis=1) + 1) // 2
    before = jnp.sum(jnp.where(columns[None, :] < column[:, None], pairs[None, :], 0), axis=1)
    earlier = (column[None, :] == column[:, None]) & (number[None, :] < number[:, None])
    place = 2 * before + jnp.sum(earlier.astype(jnp.int32), axis=1)
    places = jnp.arange(2 * most, dtype=jnp.int32)
    slot = count - jnp.sum(jnp.where(place[None, :] == places[:, None], count - number[None, :], 0), axis=1)
    ends = jnp.sum(jnp.where(columns[None, :] <= columns[:, None], pairs[None, :], 0), axis=1)
    pair_column = jnp.sum((ends[None, :] <= places[:most, None]).astype(jnp.int32), axis=1)
    pair_column = jnp.minimum(pair_column, col_blocks - 1)
    steps = (ends[-1:] + PAIRS - 1) // PAIRS
    return steps, pair_column, slot, jnp.pad(index, (0, 1)), jnp.pad(own_scales.reshape(-1), (0, 1))


def add(*terms):
    total = terms[0].astype(F32)
    for term in terms[1:]:
        total = total + term.astype(F32)
    return total.astype(BF16)


class ChipGrid:
    SIZE = 16
    CYCLE = [(0, 0), (1, 0), (2, 0), (3, 0), (3, 1), (2, 1), (1, 1), (0, 1)]

    def __init__(self):
        cycle = self.CYCLE
        n = len(cycle)
        at = {chip: i for i, chip in enumerate(cycle)}
        number = lambda z, y, c: (z * 2 + y) * 2 + c
        self.ring = []
        self.piece_rank = np.zeros((self.SIZE, self.SIZE), np.int32)
        self.rank_source = np.zeros((self.SIZE, self.SIZE), np.int32)
        for z in range(4):
            for y in range(2):
                for c in range(2):
                    me, i = number(z, y, c), at[(z, y)]
                    way = 1 if c == 0 else -1
                    self.ring.append((me, number(*cycle[(i + way) % n], c)))
                    found = [(0, 0), (0, 1)]
                    for hop in (1, 2, 3):
                        found += [(-way * hop, 0), (-way * hop, 1), (way * hop, 1), (way * hop, 0)]
                    found += [(4, 0), (4, 1)]
                    for k, (offset, dc) in enumerate(found):
                        sz, sy = cycle[(i + offset) % n]
                        self.piece_rank[me, k] = self.rank(sz ^ z, sy ^ y, dc)
                    for dz in range(4):
                        for dy in range(2):
                            for dc in range(2):
                                self.rank_source[me, self.rank(dz, dy, dc)] = number(z ^ dz, y ^ dy, c ^ dc)

    @staticmethod
    def rank(dz, dy, dc):
        return dc * 8 + dy * 4 + (dz % 2) * 2 + dz // 2

    def partner(self, x, dz, dy, dc):
        delta = (dz * 2 + dy) * 2 + dc
        return lax.ppermute(x, "expert", [(i, i ^ delta) for i in range(self.SIZE)])

    def hop(self, x):
        return lax.ppermute(x, "expert", self.ring)

    def other_core(self, x):
        return self.partner(x, 0, 0, 1)

    def other_y(self, x):
        return self.partner(x, 0, 1, 0)

    def near_z(self, x):
        return self.partner(x, 1, 0, 0)

    def far_z(self, x):
        return self.partner(x, 2, 0, 0)


def add_rows(first, last, *terms):
    return add(*[term[first:last] for term in terms])


def add_cols(first, last, first_col, last_col, *terms):
    return add(*[term[first:last, first_col:last_col] for term in terms])


def body(
    hidden_act,
    routes,
    gates,
    down_codes,
    down_scales,
    changed,
    fresh_codes,
    fresh_scales,
    block_ids,
):
    experts = lax.axis_size("expert")
    learners = lax.axis_size("learner")
    own = lax.axis_index("expert")
    own_half = lax.axis_index("learner")
    step_count, row_count, top_count, width = hidden_act.shape
    cols = down_codes.shape[2]
    routed = row_count * top_count
    row_blocks, col_blocks = width // BLK, cols // BLK
    slots_each = fresh_codes.shape[2]
    some_unchanged = changed.shape[0] < experts

    gated = (hidden_act.astype(F32) * gates[..., None]).astype(BF16).reshape(step_count, routed, width)
    flat_routes = routes.reshape(step_count, routed)
    row = jnp.arange(experts * row_count, dtype=jnp.int32)
    entry = jnp.arange(routed, dtype=jnp.int32)

    def spread(step):
        pick = (row[:, None] // row_count == flat_routes[step][None, :]) & (
            row[:, None] % row_count == entry[None, :] // top_count
        )
        out = jnp.dot(pick.astype(BF16), gated[step], preferred_element_type=F32)
        return out.astype(BF16).reshape(experts, row_count, width)

    def with_routes(step):
        tail = jnp.zeros((PAD_ROWS, width), BF16).at[0, :routed].set(flat_routes[step].astype(BF16))
        return jnp.concatenate([gated[step], tail], axis=0)

    codes = fresh_codes.reshape((-1, BLK, BLK))
    scales = down_scales[0]

    third = 2 * (col_blocks // 6)
    part_blocks = (col_blocks - 2 * third, third, third)

    def fresh_order(changed, block_ids, fresh_scales):
        first = own * slots_each
        own_ids = lax.dynamic_slice_in_dim(block_ids[:, own_half], first, slots_each, axis=1)
        return fresh_plan(own_ids, fresh_scales[:, 0], changed, col_blocks, row_blocks)

    def old(act, order):
        return old_product(act, down_codes[0], scales, order)

    def fresh(pieces, pos, plan):
        return fresh_product(pieces, pos, codes, plan, part_blocks, experts, row_count, top_count)

    if experts == ChipGrid.SIZE and learners == 1 and not some_unchanged and step_count == 2:
        grid = ChipGrid()
        together = lax.optimization_barrier
        order = jnp.asarray(grid.rank_source)[own]
        pos = jnp.asarray(grid.piece_rank)[own]
        unit = row_count

        p = [with_routes(1)]
        p.append(grid.hop(p[0]))
        q = [grid.other_core(p[0])]
        q[0], spread_old = together((q[0], spread(0)))
        q.append(grid.hop(q[0]))
        act_old = lax.all_to_all(spread_old, "expert", split_axis=0, concat_axis=0, tiled=True)
        q[1], order, pos, changed, block_ids, fresh_scales = together(
            (q[1], order, pos, changed, block_ids, fresh_scales)
        )
        plan = fresh_order(changed, block_ids, fresh_scales)

        p.append(grid.hop(p[1]))
        q.append(grid.hop(q[1]))
        q[2], act_old, plan = together((q[2], act_old, plan))

        p.append(grid.hop(p[2]))
        q.append(grid.hop(q[2]))
        keep_old, send_old = old(act_old, order)
        p[3], q[3], keep_old, send_old = together((p[3], q[3], keep_old, send_old))

        p.append(grid.hop(p[3]))
        got_old = grid.other_core(send_old)
        pieces = [p[0], q[0]]
        for k in (1, 2, 3):
            pieces += [p[k], q[k], grid.other_core(p[k]), grid.other_core(q[k])]

        cut = cols // 2 // BLK * BLK
        rows_y = add_cols(4 * unit, 8 * unit, 0, cut, keep_old, got_old)
        rows_z = jnp.concatenate(
            [add_cols(first, first + 2 * unit, cut, cols, keep_old, got_old) for first in (2 * unit, 6 * unit)]
        )
        p[4], pieces, rows_y, rows_z = together((p[4], pieces, rows_y, rows_z))
        pieces += [p[4], grid.other_core(p[4])]

        old_y = grid.other_y(rows_y)
        old_z = grid.near_z(rows_z)
        halves = fresh(pieces, pos, plan)
        old_y, old_z, halves = together((old_y, old_z, halves))

        terms = [[keep, grid.other_core(send)] for keep, send in halves]
        for term in terms:
            term.append(grid.other_y(add_rows(4 * unit, 8 * unit, *term)))
        y_terms = [keep_old[: 4 * unit, :cut], got_old[: 4 * unit, :cut], old_y]
        z_terms = [
            jnp.concatenate([term[: 2 * unit, cut:], term[4 * unit : 6 * unit, cut:]]) for term in (keep_old, got_old)
        ] + [old_z]
        near_y = grid.near_z(add_rows(2 * unit, 4 * unit, *y_terms))
        far_z = jnp.concatenate([add_rows(first, first + unit, *z_terms) for first in (unit, 3 * unit)])
        far_z = grid.far_z(far_z)
        terms[0][2], near_y, far_z = together((terms[0][2], near_y, far_z))

        y_terms = [term[: 2 * unit] for term in y_terms] + [near_y]
        z_terms = [jnp.concatenate([term[:unit], term[2 * unit : 3 * unit]]) for term in z_terms] + [far_z]
        end_y = grid.far_z(add_rows(unit, 2 * unit, *y_terms))
        end_z = grid.other_y(add_rows(unit, 2 * unit, *z_terms))
        ends = {}
        parts = len(terms)
        for phase in range(parts + 1):
            moving = {}
            if phase < parts:
                moving["near"] = grid.near_z(add_rows(2 * unit, 4 * unit, *terms[phase]))
            if phase >= 1:
                last = [term[: 2 * unit] for term in terms[phase - 1]]
                moving["end"] = grid.far_z(add_rows(unit, 2 * unit, *last))
            if phase + 1 < parts:
                moving["y"] = terms[phase + 1][2]
            if phase == 0:
                moving["old"] = (end_y, end_z)
            moving = together(moving)
            if phase < parts:
                terms[phase].append(moving["near"])
            if phase >= 1:
                ends[phase - 1] = moving["end"]
            if phase + 1 < parts:
                terms[phase + 1][2] = moving["y"]
            if phase == 0:
                end_y, end_z = moving["old"]
        old_out = [add_rows(0, unit, *y_terms, end_y), add_rows(0, unit, *z_terms, end_z)]
        new_out = [add_rows(0, unit, *terms[i], ends[i]) for i in range(parts)]
        return jnp.stack([jnp.concatenate(old_out, axis=1), jnp.concatenate(new_out, axis=1)])

    group = experts * learners
    straight = jnp.arange(group, dtype=jnp.int32)

    def joined(halves):
        return jnp.concatenate([jnp.concatenate(half, axis=0) for half in halves], axis=1)

    def combine(part):
        summed = lax.psum_scatter(part, "expert", scatter_dimension=0, tiled=True)
        return lax.all_to_all(summed, "learner", split_axis=0, concat_axis=1, tiled=True)

    def old_part(step):
        dense = lax.all_to_all(spread(step), "expert", split_axis=0, concat_axis=0, tiled=True)
        if step > 0:
            dense = jnp.where(jnp.any(changed == own), jnp.zeros_like(dense), dense)
        dense = lax.all_gather(dense, "learner", axis=1, tiled=False)
        dense = dense.reshape(group, row_count, width)
        chunks = []
        for first in range(0, group, at_once):
            act = dense[first : first + at_once]
            chunks.append(joined([old(act, straight[:at_once])]))
        return jnp.concatenate(chunks, axis=0)

    def fresh_part(step):
        everyone = lax.all_gather(with_routes(step), ("expert", "learner"), axis=0)
        chunks = []
        for first in range(0, group, at_once):
            pieces = [everyone[first + i] for i in range(at_once)]
            chunks.append(joined(fresh(pieces, straight[:at_once], plan)))
        return jnp.concatenate(chunks, axis=0)

    at_once = min(group, 16)
    plan = fresh_order(changed, block_ids, fresh_scales)
    results = [combine(old_part(0))]
    for step in range(1, step_count):
        total = fresh_part(step)
        if some_unchanged:
            total = add(total, old_part(step))
        results.append(combine(total))
    return jnp.stack(results)


def solution(mesh):
    in_specs = (
        P(None, ("groups", "expert", "learner"), None, None),
        P(None, ("groups", "expert", "learner"), None),
        P(None, ("groups", "expert", "learner"), None),
        P("expert", None, "learner"),
        P("expert", None, "learner"),
        P("groups"),
        P("groups", "learner", "expert", None, None),
        P("groups", "learner", "expert"),
        P("groups", None, None),
    )
    out_specs = P(None, ("groups", "expert", "learner"), None)
    return jax.shard_map(body, mesh=mesh, in_specs=in_specs, out_specs=out_specs, check_vma=False)
```

```python
import functools

import jax
import jax.numpy as jnp
import numpy as np
from jax import lax
from jax.experimental import pallas as pl
from jax.experimental.pallas import tpu as pltpu
from jax.sharding import PartitionSpec as P

BLK = 128
LANES = 128
PAD_ROWS = 16
PAIRS = 16
SPARE_VMEM = 3 * 1024 * 1024
F32 = jnp.float32
BF16 = jnp.bfloat16


def in_vmem(x):
    return pltpu.with_memory_space_constraint(x, pltpu.VMEM)


def in_hbm(x):
    return pltpu.with_memory_space_constraint(x, pltpu.HBM)


def prepare_kernel(experts, act_hbm, route_hbm, gate_hbm, spread_ref, piece_ref, act_ref, route_ref, gate_ref, sems):
    _, row_count, top_count, width = act_ref.shape
    routed = row_count * top_count
    arrivals = [
        pltpu.make_async_copy(source, here, sems.at[i])
        for i, (source, here) in enumerate(((act_hbm, act_ref), (route_hbm, route_ref), (gate_hbm, gate_ref)))
    ]
    for arrival in arrivals:
        arrival.start()
    for arrival in arrivals:
        arrival.wait()
    choice = lax.broadcasted_iota(jnp.int32, (top_count, routed), 0)
    entry = lax.broadcasted_iota(jnp.int32, (top_count, routed), 1)

    def gated(step):
        rows = [act_ref[step, r].astype(F32) * gate_ref[step][:, r : r + 1] for r in range(row_count)]
        return jnp.concatenate(rows, axis=0).astype(BF16)

    def route_row(step):
        routes = route_ref[step].astype(F32)
        wide = jnp.zeros((top_count, routed), F32)
        for r in range(row_count):
            wide = jnp.where(entry // top_count == r, routes[:, r : r + 1], wide)
        return jnp.sum(jnp.where(entry % top_count == choice, wide, 0.0), axis=0, keepdims=True)

    piece_ref[0:routed, :] = gated(1)
    piece_ref[routed:, :] = jnp.zeros((PAD_ROWS, width), BF16)
    top = lax.broadcasted_iota(jnp.int32, (PAD_ROWS, routed), 0) == 0
    piece_ref[routed:, 0:routed] = jnp.where(top, route_row(1), 0.0).astype(BF16)
    long_row = lax.broadcasted_iota(jnp.int32, (experts * row_count, routed), 0)
    long_entry = lax.broadcasted_iota(jnp.int32, (experts * row_count, routed), 1)
    match = (long_row % row_count == long_entry // top_count) & (
        (long_row // row_count).astype(F32) == route_row(0)
    )
    pick = jnp.where(match, 1.0, 0.0).astype(BF16)
    spread = jnp.dot(pick, gated(0), preferred_element_type=F32).astype(BF16)
    for e in range(experts):
        spread_ref[e] = spread[e * row_count : (e + 1) * row_count]


def prepare(hidden_act, routes, gates, experts):
    _, row_count, top_count, width = hidden_act.shape
    whole = pl.BlockSpec(memory_space=pltpu.VMEM)
    return pl.pallas_call(
        functools.partial(prepare_kernel, experts),
        in_specs=[pl.BlockSpec(memory_space=pl.ANY)] * 3,
        out_specs=[whole] * 2,
        scratch_shapes=[
            pltpu.VMEM(hidden_act.shape, BF16),
            pltpu.VMEM((2, top_count, row_count), jnp.int32),
            pltpu.VMEM((2, top_count, row_count), F32),
            pltpu.SemaphoreType.DMA((3,)),
        ],
        out_shape=[
            pltpu.VMEM((experts, row_count, width), BF16),
            pltpu.VMEM((row_count * top_count + PAD_ROWS, width), BF16),
        ],
        compiler_params=pltpu.CompilerParams(vmem_limit_bytes=6 * SPARE_VMEM),
        cost_estimate=pl.CostEstimate(flops=0, bytes_accessed=0, transcendentals=0),
        name="prepare",
    )(*[in_hbm(x) for x in (hidden_act, routes.transpose(0, 2, 1), gates.transpose(0, 2, 1))])


def old_kernel(order_ref, scale_ref, act_ref, code_hbm, keep_ref, send_ref, act_scratch, code_buf, code_sem):
    groups, group_rows, width = act_ref.shape
    chunks, _, chunk_cols = code_buf.shape

    def arrival(c):
        columns = pl.ds(c * chunk_cols, chunk_cols)
        return pltpu.make_async_copy(code_hbm.at[:, columns], code_buf.at[c], code_sem.at[c])

    for c in range(chunks):
        arrival(c).start()
    for g in range(groups):
        act_scratch[g * group_rows : (g + 1) * group_rows, :] = act_ref[order_ref[g]]
    act = act_scratch[...]
    half = act.shape[0] // 2
    per_chunk = chunk_cols // BLK
    for c in range(chunks):
        arrival(c).wait()
        for t in range(0, per_chunk, 2):
            rows = []
            for i in range(width // BLK):
                pair = []
                for j in range(t, t + 2):
                    block = code_buf[c, i * BLK : (i + 1) * BLK, j * BLK : (j + 1) * BLK]
                    scale = scale_ref[i * chunks * per_chunk + c * per_chunk + j]
                    pair.append((block.astype(F32) * scale).astype(BF16))
                rows.append(jnp.concatenate(pair, axis=1))
            weight = jnp.concatenate(rows, axis=0)
            product = jnp.dot(act, weight, preferred_element_type=F32).astype(BF16)
            at = slice(c * chunk_cols + t * BLK, c * chunk_cols + (t + 2) * BLK)
            keep_ref[:, at] = product[:half]
            send_ref[:, at] = product[half:]


def halves_of(rows, part_blocks):
    shapes = []
    for blocks in part_blocks:
        shapes += [pltpu.VMEM((rows // 2, blocks * BLK), BF16)] * 2
    return shapes


def old_product(act, codes, scales, order):
    groups, group_rows, width = act.shape
    rows, cols = groups * group_rows, codes.shape[1]
    chunks = cols // (14 * BLK)
    whole = pl.BlockSpec(memory_space=pltpu.VMEM)
    return pl.pallas_call(
        old_kernel,
        grid_spec=pltpu.PrefetchScalarGridSpec(
            num_scalar_prefetch=2,
            grid=(),
            in_specs=[whole, pl.BlockSpec(memory_space=pl.ANY)],
            out_specs=[whole] * 2,
            scratch_shapes=[
                pltpu.VMEM((rows, width), BF16),
                pltpu.VMEM((chunks, width, cols // chunks), BF16),
                pltpu.SemaphoreType.DMA((chunks,)),
            ],
        ),
        out_shape=halves_of(rows, (cols // BLK,)),
        compiler_params=pltpu.CompilerParams(vmem_limit_bytes=2 * (rows + cols) * width + SPARE_VMEM),
        cost_estimate=pl.CostEstimate(flops=0, bytes_accessed=0, transcendentals=0),
        name="old_product",
    )(order, scales.reshape(-1), in_vmem(act), in_hbm(codes))


def fresh_kernel(
    n_pieces, experts, row_count, top_count, part_blocks,
    pos_ref, steps_ref, column_ref, slot_ref, index_ref, scale_ref,
    *refs,
):
    pieces, code_ref = refs[:n_pieces], refs[n_pieces]
    outs, dense, total = refs[n_pieces + 1 : -2], refs[-2], refs[-1]
    width = pieces[0].shape[1]
    row_blocks = width // BLK
    routed = row_count * top_count
    slots = code_ref.shape[0]
    half = dense.shape[1] // 2

    row = lax.broadcasted_iota(jnp.int32, (experts * row_count, routed), 0)
    col = lax.broadcasted_iota(jnp.int32, (experts * row_count, routed), 1)
    same_row = row % row_count == col // top_count
    expert = (row // row_count).astype(F32)
    for i in range(n_pieces):
        route = pieces[i][routed : routed + PAD_ROWS, 0:routed].astype(F32)[0:1, :]
        pick = jnp.where(same_row & (expert == route), 1.0, 0.0).astype(BF16)
        spread = jnp.dot(pick, pieces[i][0:routed, :], preferred_element_type=F32).astype(BF16)
        at = pl.ds(pl.multiple_of(pos_ref[i] * row_count, row_count), row_count)
        for e in range(experts):
            for b in range(row_blocks):
                dense[e * row_blocks + b, at, :] = spread[
                    e * row_count : (e + 1) * row_count, b * BLK : (b + 1) * BLK
                ]

    def clear(j, carry):
        total[j] = jnp.zeros(total.shape[1:], F32)
        return carry

    def some_pairs(t, carry):
        products = []
        for u in range(PAIRS):
            number = t * PAIRS + u
            left, right = [], []
            for q in range(2):
                slot = slot_ref[2 * number + q]
                block = code_ref[jnp.minimum(slot, slots - 1)]
                right.append((block.astype(F32) * scale_ref[slot]).astype(BF16))
                left.append(dense[index_ref[slot]])
            left, right = jnp.concatenate(left, axis=1), jnp.concatenate(right, axis=0)
            products.append(jnp.dot(left, right, preferred_element_type=F32))
        for u in range(PAIRS):
            total[column_ref[t * PAIRS + u]] += products[u]
        return carry

    lax.fori_loop(0, total.shape[0], clear, 0)
    lax.fori_loop(0, steps_ref[0], some_pairs, 0)
    first = 0
    for part, blocks in enumerate(part_blocks):
        for j in range(blocks):
            done = total[first + j].astype(BF16)
            outs[2 * part][:, j * BLK : (j + 1) * BLK] = done[:half]
            outs[2 * part + 1][:, j * BLK : (j + 1) * BLK] = done[half:]
        first += blocks


def fresh_product(pieces, pos, codes, plan, part_blocks, experts, row_count, top_count):
    n_pieces = len(pieces)
    rows, cols = n_pieces * row_count, sum(part_blocks) * BLK
    width = pieces[0].shape[1]
    slots = codes.shape[0]
    whole = pl.BlockSpec(memory_space=pltpu.VMEM)
    outs = pl.pallas_call(
        functools.partial(fresh_kernel, n_pieces, experts, row_count, top_count, part_blocks),
        grid_spec=pltpu.PrefetchScalarGridSpec(
            num_scalar_prefetch=6,
            grid=(),
            in_specs=[whole] * (n_pieces + 1),
            out_specs=[whole] * (2 * len(part_blocks)),
            scratch_shapes=[
                pltpu.VMEM((experts * (width // BLK), rows, BLK), BF16),
                pltpu.VMEM((sum(part_blocks), rows, BLK), F32),
            ],
        ),
        out_shape=halves_of(rows, part_blocks),
        compiler_params=pltpu.CompilerParams(
            vmem_limit_bytes=2 * experts * width * rows + 4 * rows * cols + SPARE_VMEM
        ),
        cost_estimate=pl.CostEstimate(flops=0, bytes_accessed=0, transcendentals=0),
        name="fresh_product",
    )(pos, *plan, *[in_vmem(piece) for piece in pieces], in_vmem(codes))
    return [outs[2 * i : 2 * i + 2] for i in range(len(part_blocks))]


def fresh_plan(own_ids, own_scales, changed, col_blocks, row_blocks):
    slots_each = own_ids.shape[1]
    ids = own_ids.reshape(-1)
    count = ids.shape[0]
    column = ids % col_blocks
    index = jnp.repeat(changed, slots_each) * row_blocks + ids // col_blocks
    number = jnp.arange(count, dtype=jnp.int32)
    columns = jnp.arange(col_blocks, dtype=jnp.int32)
    most = -(-(count // 2 + (col_blocks + 1) // 2) // PAIRS) * PAIRS
    pairs = (jnp.sum((column[None, :] == columns[:, None]).astype(jnp.int32), axis=1) + 1) // 2
    before = jnp.sum(jnp.where(columns[None, :] < column[:, None], pairs[None, :], 0), axis=1)
    earlier = (column[None, :] == column[:, None]) & (number[None, :] < number[:, None])
    place = 2 * before + jnp.sum(earlier.astype(jnp.int32), axis=1)
    places = jnp.arange(2 * most, dtype=jnp.int32)
    slot = count - jnp.sum(jnp.where(place[None, :] == places[:, None], count - number[None, :], 0), axis=1)
    ends = jnp.sum(jnp.where(columns[None, :] <= columns[:, None], pairs[None, :], 0), axis=1)
    pair_column = jnp.sum((ends[None, :] <= places[:most, None]).astype(jnp.int32), axis=1)
    pair_column = jnp.minimum(pair_column, col_blocks - 1)
    steps = (ends[-1:] + PAIRS - 1) // PAIRS
    return steps, pair_column, slot, jnp.pad(index, (0, 1)), jnp.pad(own_scales.reshape(-1), (0, 1))


def add(*terms):
    total = terms[0].astype(F32)
    for term in terms[1:]:
        total = total + term.astype(F32)
    return total.astype(BF16)


class ChipGrid:
    SIZE = 16
    CYCLE = [(0, 0), (1, 0), (2, 0), (3, 0), (3, 1), (2, 1), (1, 1), (0, 1)]

    def __init__(self):
        cycle = self.CYCLE
        n = len(cycle)
        at = {chip: i for i, chip in enumerate(cycle)}
        number = lambda z, y, c: (z * 2 + y) * 2 + c
        self.ring = []
        self.piece_rank = np.zeros((self.SIZE, self.SIZE), np.int32)
        self.rank_source = np.zeros((self.SIZE, self.SIZE), np.int32)
        for z in range(4):
            for y in range(2):
                for c in range(2):
                    me, i = number(z, y, c), at[(z, y)]
                    way = 1 if c == 0 else -1
                    self.ring.append((me, number(*cycle[(i + way) % n], c)))
                    found = [(0, 0), (0, 1)]
                    for hop in (1, 2, 3):
                        found += [(-way * hop, 0), (-way * hop, 1), (way * hop, 1), (way * hop, 0)]
                    found += [(4, 0), (4, 1)]
                    for k, (offset, dc) in enumerate(found):
                        sz, sy = cycle[(i + offset) % n]
                        self.piece_rank[me, k] = self.rank(sz ^ z, sy ^ y, dc)
                    for dz in range(4):
                        for dy in range(2):
                            for dc in range(2):
                                self.rank_source[me, self.rank(dz, dy, dc)] = number(z ^ dz, y ^ dy, c ^ dc)

    @staticmethod
    def rank(dz, dy, dc):
        return dc * 8 + dy * 4 + (dz % 2) * 2 + dz // 2

    def partner(self, x, dz, dy, dc):
        delta = (dz * 2 + dy) * 2 + dc
        return lax.ppermute(x, "expert", [(i, i ^ delta) for i in range(self.SIZE)])

    def hop(self, x):
        return lax.ppermute(x, "expert", self.ring)

    def other_core(self, x):
        return self.partner(x, 0, 0, 1)

    def other_y(self, x):
        return self.partner(x, 0, 1, 0)

    def near_z(self, x):
        return self.partner(x, 1, 0, 0)

    def far_z(self, x):
        return self.partner(x, 2, 0, 0)


def add_rows(first, last, *terms):
    return add(*[term[first:last] for term in terms])


def add_cols(first, last, first_col, last_col, *terms):
    return add(*[term[first:last, first_col:last_col] for term in terms])


def body(
    hidden_act,
    routes,
    gates,
    down_codes,
    down_scales,
    changed,
    fresh_codes,
    fresh_scales,
    block_ids,
):
    experts = lax.axis_size("expert")
    learners = lax.axis_size("learner")
    own = lax.axis_index("expert")
    own_half = lax.axis_index("learner")
    step_count, row_count, top_count, width = hidden_act.shape
    cols = down_codes.shape[2]
    routed = row_count * top_count
    row_blocks, col_blocks = width // BLK, cols // BLK
    slots_each = fresh_codes.shape[2]
    some_unchanged = changed.shape[0] < experts

    gated = (hidden_act.astype(F32) * gates[..., None]).astype(BF16).reshape(step_count, routed, width)
    flat_routes = routes.reshape(step_count, routed)
    row = jnp.arange(experts * row_count, dtype=jnp.int32)
    entry = jnp.arange(routed, dtype=jnp.int32)

    def spread(step):
        pick = (row[:, None] // row_count == flat_routes[step][None, :]) & (
            row[:, None] % row_count == entry[None, :] // top_count
        )
        out = jnp.dot(pick.astype(BF16), gated[step], preferred_element_type=F32)
        return out.astype(BF16).reshape(experts, row_count, width)

    def with_routes(step):
        tail = jnp.zeros((PAD_ROWS, width), BF16).at[0, :routed].set(flat_routes[step].astype(BF16))
        return jnp.concatenate([gated[step], tail], axis=0)

    codes = fresh_codes.reshape((-1, BLK, BLK))
    scales = down_scales[0]

    third = 2 * (col_blocks // 6)
    part_blocks = (col_blocks - 2 * third, third, third)

    def fresh_order(changed, block_ids, fresh_scales):
        first = own * slots_each
        own_ids = lax.dynamic_slice_in_dim(block_ids[:, own_half], first, slots_each, axis=1)
        return fresh_plan(own_ids, fresh_scales[:, 0], changed, col_blocks, row_blocks)

    def old(act, order):
        return old_product(act, down_codes[0], scales, order)

    def fresh(pieces, pos, plan):
        return fresh_product(pieces, pos, codes, plan, part_blocks, experts, row_count, top_count)

    if experts == ChipGrid.SIZE and learners == 1 and not some_unchanged and step_count == 2:
        grid = ChipGrid()
        together = lax.optimization_barrier
        order = jnp.asarray(grid.rank_source)[own]
        pos = jnp.asarray(grid.piece_rank)[own]
        unit = row_count

        spread_old, first_piece = prepare(hidden_act, routes, gates, experts)
        p = [first_piece]
        p.append(grid.hop(p[0]))
        q = [grid.other_core(p[0])]
        q[0], spread_old = together((q[0], spread_old))
        q.append(grid.hop(q[0]))
        act_old = lax.all_to_all(spread_old, "expert", split_axis=0, concat_axis=0, tiled=True)
        q[1], order, pos, changed, block_ids, fresh_scales = together(
            (q[1], order, pos, changed, block_ids, fresh_scales)
        )
        plan = fresh_order(changed, block_ids, fresh_scales)

        p.append(grid.hop(p[1]))
        q.append(grid.hop(q[1]))
        q[2], act_old, plan = together((q[2], act_old, plan))

        p.append(grid.hop(p[2]))
        q.append(grid.hop(q[2]))
        keep_old, send_old = old(act_old, order)
        p[3], q[3], keep_old, send_old = together((p[3], q[3], keep_old, send_old))

        p.append(grid.hop(p[3]))
        got_old = grid.other_core(send_old)
        pieces = [p[0], q[0]]
        for k in (1, 2, 3):
            pieces += [p[k], q[k], grid.other_core(p[k]), grid.other_core(q[k])]

        cut = cols // 2 // BLK * BLK
        rows_y = add_cols(4 * unit, 8 * unit, 0, cut, keep_old, got_old)
        rows_z = jnp.concatenate(
            [add_cols(first, first + 2 * unit, cut, cols, keep_old, got_old) for first in (2 * unit, 6 * unit)]
        )
        pieces, rows_y, rows_z = together((pieces, rows_y, rows_z))
        pieces += [p[4], grid.other_core(p[4])]

        old_y = grid.other_y(rows_y)
        old_z = grid.near_z(rows_z)
        halves = fresh(pieces, pos, plan)
        old_y, old_z, halves = together((old_y, old_z, halves))

        terms = [[keep, grid.other_core(send)] for keep, send in halves]
        for term in terms:
            term.append(grid.other_y(add_rows(4 * unit, 8 * unit, *term)))
        y_terms = [keep_old[: 4 * unit, :cut], got_old[: 4 * unit, :cut], old_y]
        z_terms = [
            jnp.concatenate([term[: 2 * unit, cut:], term[4 * unit : 6 * unit, cut:]]) for term in (keep_old, got_old)
        ] + [old_z]
        near_y = grid.near_z(add_rows(2 * unit, 4 * unit, *y_terms))
        far_z = jnp.concatenate([add_rows(first, first + unit, *z_terms) for first in (unit, 3 * unit)])
        far_z = grid.far_z(far_z)
        terms[0][2], near_y, far_z = together((terms[0][2], near_y, far_z))

        y_terms = [term[: 2 * unit] for term in y_terms] + [near_y]
        z_terms = [jnp.concatenate([term[:unit], term[2 * unit : 3 * unit]]) for term in z_terms] + [far_z]
        end_y = grid.far_z(add_rows(unit, 2 * unit, *y_terms))
        end_z = grid.other_y(add_rows(unit, 2 * unit, *z_terms))
        ends = {}
        parts = len(terms)
        for phase in range(parts + 1):
            moving = {}
            if phase < parts:
                moving["near"] = grid.near_z(add_rows(2 * unit, 4 * unit, *terms[phase]))
            if phase >= 1:
                last = [term[: 2 * unit] for term in terms[phase - 1]]
                moving["end"] = grid.far_z(add_rows(unit, 2 * unit, *last))
            if phase + 1 < parts:
                moving["y"] = terms[phase + 1][2]
            if phase == 0:
                moving["old"] = (end_y, end_z)
            moving = together(moving)
            if phase < parts:
                terms[phase].append(moving["near"])
            if phase >= 1:
                ends[phase - 1] = moving["end"]
            if phase + 1 < parts:
                terms[phase + 1][2] = moving["y"]
            if phase == 0:
                end_y, end_z = moving["old"]
        old_out = [add_rows(0, unit, *y_terms, end_y), add_rows(0, unit, *z_terms, end_z)]
        new_out = [add_rows(0, unit, *terms[i], ends[i]) for i in range(parts)]
        return jnp.stack([jnp.concatenate(old_out, axis=1), jnp.concatenate(new_out, axis=1)])

    group = experts * learners
    straight = jnp.arange(group, dtype=jnp.int32)

    def joined(halves):
        return jnp.concatenate([jnp.concatenate(half, axis=0) for half in halves], axis=1)

    def combine(part):
        summed = lax.psum_scatter(part, "expert", scatter_dimension=0, tiled=True)
        return lax.all_to_all(summed, "learner", split_axis=0, concat_axis=1, tiled=True)

    def old_part(step):
        dense = lax.all_to_all(spread(step), "expert", split_axis=0, concat_axis=0, tiled=True)
        if step > 0:
            dense = jnp.where(jnp.any(changed == own), jnp.zeros_like(dense), dense)
        dense = lax.all_gather(dense, "learner", axis=1, tiled=False)
        dense = dense.reshape(group, row_count, width)
        chunks = []
        for first in range(0, group, at_once):
            act = dense[first : first + at_once]
            chunks.append(joined([old(act, straight[:at_once])]))
        return jnp.concatenate(chunks, axis=0)

    def fresh_part(step):
        everyone = lax.all_gather(with_routes(step), ("expert", "learner"), axis=0)
        chunks = []
        for first in range(0, group, at_once):
            pieces = [everyone[first + i] for i in range(at_once)]
            chunks.append(joined(fresh(pieces, straight[:at_once], plan)))
        return jnp.concatenate(chunks, axis=0)

    at_once = min(group, 16)
    plan = fresh_order(changed, block_ids, fresh_scales)
    results = [combine(old_part(0))]
    for step in range(1, step_count):
        total = fresh_part(step)
        if some_unchanged:
            total = add(total, old_part(step))
        results.append(combine(total))
    return jnp.stack(results)


def solution(mesh):
    in_specs = (
        P(None, ("groups", "expert", "learner"), None, None),
        P(None, ("groups", "expert", "learner"), None),
        P(None, ("groups", "expert", "learner"), None),
        P("expert", None, "learner"),
        P("expert", None, "learner"),
        P("groups"),
        P("groups", "learner", "expert", None, None),
        P("groups", "learner", "expert"),
        P("groups", None, None),
    )
    out_specs = P(None, ("groups", "expert", "learner"), None)
    return jax.shard_map(body, mesh=mesh, in_specs=in_specs, out_specs=out_specs, check_vma=False)
```

```python
import functools

import jax
import jax.numpy as jnp
import numpy as np
from jax import lax
from jax.experimental import pallas as pl
from jax.experimental.pallas import tpu as pltpu
from jax.sharding import PartitionSpec as P

BLK = 128
LANES = 128
PAD_ROWS = 16
PAIRS = 24
SPARE_VMEM = 8 * 1024 * 1024
F32 = jnp.float32
BF16 = jnp.bfloat16


def in_vmem(x):
    return pltpu.with_memory_space_constraint(x, pltpu.VMEM)


def in_hbm(x):
    return pltpu.with_memory_space_constraint(x, pltpu.HBM)


def prepare_kernel(experts, act_hbm, route_hbm, gate_hbm, spread_ref, piece_ref, act_ref, route_ref, gate_ref, sems):
    _, row_count, top_count, width = act_ref.shape
    routed = row_count * top_count
    arrivals = [
        pltpu.make_async_copy(source, here, sems.at[i])
        for i, (source, here) in enumerate(((act_hbm, act_ref), (route_hbm, route_ref), (gate_hbm, gate_ref)))
    ]
    for arrival in arrivals:
        arrival.start()
    for arrival in arrivals:
        arrival.wait()
    choice = lax.broadcasted_iota(jnp.int32, (top_count, routed), 0)
    entry = lax.broadcasted_iota(jnp.int32, (top_count, routed), 1)

    def gated(step):
        rows = [act_ref[step, r].astype(F32) * gate_ref[step][:, r : r + 1] for r in range(row_count)]
        return jnp.concatenate(rows, axis=0).astype(BF16)

    def route_row(step):
        routes = route_ref[step].astype(F32)
        wide = jnp.zeros((top_count, routed), F32)
        for r in range(row_count):
            wide = jnp.where(entry // top_count == r, routes[:, r : r + 1], wide)
        return jnp.sum(jnp.where(entry % top_count == choice, wide, 0.0), axis=0, keepdims=True)

    piece_ref[0:routed, :] = gated(1)
    piece_ref[routed:, :] = jnp.zeros((PAD_ROWS, width), BF16)
    top = lax.broadcasted_iota(jnp.int32, (PAD_ROWS, routed), 0) == 0
    piece_ref[routed:, 0:routed] = jnp.where(top, route_row(1), 0.0).astype(BF16)
    long_row = lax.broadcasted_iota(jnp.int32, (experts * row_count, routed), 0)
    long_entry = lax.broadcasted_iota(jnp.int32, (experts * row_count, routed), 1)
    match = (long_row % row_count == long_entry // top_count) & (
        (long_row // row_count).astype(F32) == route_row(0)
    )
    pick = jnp.where(match, 1.0, 0.0).astype(BF16)
    spread = jnp.dot(pick, gated(0), preferred_element_type=F32).astype(BF16)
    for e in range(experts):
        spread_ref[e] = spread[e * row_count : (e + 1) * row_count]


def prepare(hidden_act, routes, gates, experts):
    _, row_count, top_count, width = hidden_act.shape
    whole = pl.BlockSpec(memory_space=pltpu.VMEM)
    return pl.pallas_call(
        functools.partial(prepare_kernel, experts),
        in_specs=[pl.BlockSpec(memory_space=pl.ANY)] * 3,
        out_specs=[whole] * 2,
        scratch_shapes=[
            pltpu.VMEM(hidden_act.shape, BF16),
            pltpu.VMEM((2, top_count, row_count), jnp.int32),
            pltpu.VMEM((2, top_count, row_count), F32),
            pltpu.SemaphoreType.DMA((3,)),
        ],
        out_shape=[
            pltpu.VMEM((experts, row_count, width), BF16),
            pltpu.VMEM((row_count * top_count + PAD_ROWS, width), BF16),
        ],
        compiler_params=pltpu.CompilerParams(vmem_limit_bytes=2 * SPARE_VMEM),
        cost_estimate=pl.CostEstimate(flops=0, bytes_accessed=0, transcendentals=0),
        name="prepare",
    )(*[in_hbm(x) for x in (hidden_act, routes.transpose(0, 2, 1), gates.transpose(0, 2, 1))])


def old_kernel(order_ref, scale_ref, act_ref, code_hbm, keep_ref, send_ref, act_scratch, code_buf, code_sem):
    groups, group_rows, width = act_ref.shape
    chunks, _, chunk_cols = code_buf.shape

    def arrival(c):
        columns = pl.ds(c * chunk_cols, chunk_cols)
        return pltpu.make_async_copy(code_hbm.at[:, columns], code_buf.at[c], code_sem.at[c])

    for c in range(chunks):
        arrival(c).start()
    for g in range(groups):
        act_scratch[g * group_rows : (g + 1) * group_rows, :] = act_ref[order_ref[g]]
    act = act_scratch[...]
    half = act.shape[0] // 2
    per_chunk = chunk_cols // BLK
    for c in range(chunks):
        arrival(c).wait()
        for t in range(0, per_chunk, 2):
            rows = []
            for i in range(width // BLK):
                pair = []
                for j in range(t, t + 2):
                    block = code_buf[c, i * BLK : (i + 1) * BLK, j * BLK : (j + 1) * BLK]
                    scale = scale_ref[i * chunks * per_chunk + c * per_chunk + j]
                    pair.append((block.astype(F32) * scale).astype(BF16))
                rows.append(jnp.concatenate(pair, axis=1))
            weight = jnp.concatenate(rows, axis=0)
            product = jnp.dot(act, weight, preferred_element_type=F32).astype(BF16)
            at = slice(c * chunk_cols + t * BLK, c * chunk_cols + (t + 2) * BLK)
            keep_ref[:, at] = product[:half]
            send_ref[:, at] = product[half:]


def halves_of(rows, part_blocks):
    shapes = []
    for blocks in part_blocks:
        shapes += [pltpu.VMEM((rows // 2, blocks * BLK), BF16)] * 2
    return shapes


def old_product(act, codes, scales, order):
    groups, group_rows, width = act.shape
    rows, cols = groups * group_rows, codes.shape[1]
    chunks = cols // (14 * BLK)
    whole = pl.BlockSpec(memory_space=pltpu.VMEM)
    return pl.pallas_call(
        old_kernel,
        grid_spec=pltpu.PrefetchScalarGridSpec(
            num_scalar_prefetch=2,
            grid=(),
            in_specs=[whole, pl.BlockSpec(memory_space=pl.ANY)],
            out_specs=[whole] * 2,
            scratch_shapes=[
                pltpu.VMEM((rows, width), BF16),
                pltpu.VMEM((chunks, width, cols // chunks), BF16),
                pltpu.SemaphoreType.DMA((chunks,)),
            ],
        ),
        out_shape=halves_of(rows, (cols // BLK,)),
        compiler_params=pltpu.CompilerParams(vmem_limit_bytes=2 * (rows + cols) * width + SPARE_VMEM),
        cost_estimate=pl.CostEstimate(flops=0, bytes_accessed=0, transcendentals=0),
        name="old_product",
    )(order, scales.reshape(-1), in_vmem(act), in_hbm(codes))


def fresh_kernel(
    n_pieces, experts, row_count, top_count, part_blocks,
    pos_ref, steps_ref, column_ref, slot_ref, index_ref, scale_ref,
    *refs,
):
    pieces, code_ref = refs[:n_pieces], refs[n_pieces]
    outs, dense, total = refs[n_pieces + 1 : -2], refs[-2], refs[-1]
    width = pieces[0].shape[1]
    row_blocks = width // BLK
    routed = row_count * top_count
    slots = code_ref.shape[0]
    half = dense.shape[1] // 2

    row = lax.broadcasted_iota(jnp.int32, (experts * row_count, routed), 0)
    col = lax.broadcasted_iota(jnp.int32, (experts * row_count, routed), 1)
    same_row = row % row_count == col // top_count
    expert = (row // row_count).astype(F32)
    for i in range(n_pieces):
        route = pieces[i][routed : routed + PAD_ROWS, 0:routed].astype(F32)[0:1, :]
        pick = jnp.where(same_row & (expert == route), 1.0, 0.0).astype(BF16)
        spread = jnp.dot(pick, pieces[i][0:routed, :], preferred_element_type=F32).astype(BF16)
        at = pl.ds(pl.multiple_of(pos_ref[i] * row_count, row_count), row_count)
        for e in range(experts):
            for b in range(row_blocks):
                dense[e * row_blocks + b, at, :] = spread[
                    e * row_count : (e + 1) * row_count, b * BLK : (b + 1) * BLK
                ]

    def clear(j, carry):
        total[j] = jnp.zeros(total.shape[1:], F32)
        return carry

    def some_pairs(t, carry):
        products = []
        for u in range(PAIRS):
            number = t * PAIRS + u
            left, right = [], []
            for q in range(2):
                slot = slot_ref[2 * number + q]
                block = code_ref[jnp.minimum(slot, slots - 1)]
                right.append((block.astype(F32) * scale_ref[slot]).astype(BF16))
                left.append(dense[index_ref[slot]])
            left, right = jnp.concatenate(left, axis=1), jnp.concatenate(right, axis=0)
            products.append(jnp.dot(left, right, preferred_element_type=F32))
        for u in range(PAIRS):
            total[column_ref[t * PAIRS + u]] += products[u]
        return carry

    lax.fori_loop(0, total.shape[0], clear, 0)
    lax.fori_loop(0, steps_ref[0], some_pairs, 0)
    first = 0
    for part, blocks in enumerate(part_blocks):
        for j in range(blocks):
            done = total[first + j].astype(BF16)
            outs[2 * part][:, j * BLK : (j + 1) * BLK] = done[:half]
            outs[2 * part + 1][:, j * BLK : (j + 1) * BLK] = done[half:]
        first += blocks


def fresh_product(pieces, pos, codes, plan, part_blocks, experts, row_count, top_count):
    n_pieces = len(pieces)
    rows, cols = n_pieces * row_count, sum(part_blocks) * BLK
    width = pieces[0].shape[1]
    slots = codes.shape[0]
    whole = pl.BlockSpec(memory_space=pltpu.VMEM)
    outs = pl.pallas_call(
        functools.partial(fresh_kernel, n_pieces, experts, row_count, top_count, part_blocks),
        grid_spec=pltpu.PrefetchScalarGridSpec(
            num_scalar_prefetch=6,
            grid=(),
            in_specs=[whole] * (n_pieces + 1),
            out_specs=[whole] * (2 * len(part_blocks)),
            scratch_shapes=[
                pltpu.VMEM((experts * (width // BLK), rows, BLK), BF16),
                pltpu.VMEM((sum(part_blocks), rows, BLK), F32),
            ],
        ),
        out_shape=halves_of(rows, part_blocks),
        compiler_params=pltpu.CompilerParams(
            vmem_limit_bytes=2 * experts * width * rows + 4 * rows * cols + SPARE_VMEM
        ),
        cost_estimate=pl.CostEstimate(flops=0, bytes_accessed=0, transcendentals=0),
        name="fresh_product",
    )(pos, *plan, *[in_vmem(piece) for piece in pieces], in_vmem(codes))
    return [outs[2 * i : 2 * i + 2] for i in range(len(part_blocks))]


def fresh_plan(own_ids, own_scales, changed, col_blocks, row_blocks):
    slots_each = own_ids.shape[1]
    ids = own_ids.reshape(-1)
    count = ids.shape[0]
    column = ids % col_blocks
    index = jnp.repeat(changed, slots_each) * row_blocks + ids // col_blocks
    number = jnp.arange(count, dtype=jnp.int32)
    columns = jnp.arange(col_blocks, dtype=jnp.int32)
    most = -(-(count // 2 + (col_blocks + 1) // 2) // PAIRS) * PAIRS
    pairs = (jnp.sum((column[None, :] == columns[:, None]).astype(jnp.int32), axis=1) + 1) // 2
    before = jnp.sum(jnp.where(columns[None, :] < column[:, None], pairs[None, :], 0), axis=1)
    earlier = (column[None, :] == column[:, None]) & (number[None, :] < number[:, None])
    place = 2 * before + jnp.sum(earlier.astype(jnp.int32), axis=1)
    places = jnp.arange(2 * most, dtype=jnp.int32)
    slot = count - jnp.sum(jnp.where(place[None, :] == places[:, None], count - number[None, :], 0), axis=1)
    ends = jnp.sum(jnp.where(columns[None, :] <= columns[:, None], pairs[None, :], 0), axis=1)
    pair_column = jnp.sum((ends[None, :] <= places[:most, None]).astype(jnp.int32), axis=1)
    pair_column = jnp.minimum(pair_column, col_blocks - 1)
    steps = (ends[-1:] + PAIRS - 1) // PAIRS
    return steps, pair_column, slot, jnp.pad(index, (0, 1)), jnp.pad(own_scales.reshape(-1), (0, 1))


def add(*terms):
    total = terms[0].astype(F32)
    for term in terms[1:]:
        total = total + term.astype(F32)
    return total.astype(BF16)


class ChipGrid:
    SIZE = 16
    CYCLE = [(0, 0), (1, 0), (2, 0), (3, 0), (3, 1), (2, 1), (1, 1), (0, 1)]

    def __init__(self):
        cycle = self.CYCLE
        n = len(cycle)
        at = {chip: i for i, chip in enumerate(cycle)}
        number = lambda z, y, c: (z * 2 + y) * 2 + c
        self.ring = []
        self.piece_rank = np.zeros((self.SIZE, self.SIZE), np.int32)
        self.rank_source = np.zeros((self.SIZE, self.SIZE), np.int32)
        for z in range(4):
            for y in range(2):
                for c in range(2):
                    me, i = number(z, y, c), at[(z, y)]
                    way = 1 if c == 0 else -1
                    self.ring.append((me, number(*cycle[(i + way) % n], c)))
                    found = [(0, 0), (0, 1)]
                    for hop in (1, 2, 3):
                        found += [(-way * hop, 0), (-way * hop, 1), (way * hop, 1), (way * hop, 0)]
                    found += [(4, 0), (4, 1)]
                    for k, (offset, dc) in enumerate(found):
                        sz, sy = cycle[(i + offset) % n]
                        self.piece_rank[me, k] = self.rank(sz ^ z, sy ^ y, dc)
                    for dz in range(4):
                        for dy in range(2):
                            for dc in range(2):
                                self.rank_source[me, self.rank(dz, dy, dc)] = number(z ^ dz, y ^ dy, c ^ dc)

    @staticmethod
    def rank(dz, dy, dc):
        return dc * 8 + dy * 4 + (dz % 2) * 2 + dz // 2

    def partner(self, x, dz, dy, dc):
        delta = (dz * 2 + dy) * 2 + dc
        return lax.ppermute(x, "expert", [(i, i ^ delta) for i in range(self.SIZE)])

    def hop(self, x):
        return lax.ppermute(x, "expert", self.ring)

    def other_core(self, x):
        return self.partner(x, 0, 0, 1)

    def other_y(self, x):
        return self.partner(x, 0, 1, 0)

    def near_z(self, x):
        return self.partner(x, 1, 0, 0)

    def far_z(self, x):
        return self.partner(x, 2, 0, 0)


def add_rows(first, last, *terms):
    return add(*[term[first:last] for term in terms])


def add_cols(first, last, first_col, last_col, *terms):
    return add(*[term[first:last, first_col:last_col] for term in terms])


def body(
    hidden_act,
    routes,
    gates,
    down_codes,
    down_scales,
    changed,
    fresh_codes,
    fresh_scales,
    block_ids,
):
    experts = lax.axis_size("expert")
    learners = lax.axis_size("learner")
    own = lax.axis_index("expert")
    own_half = lax.axis_index("learner")
    step_count, row_count, top_count, width = hidden_act.shape
    cols = down_codes.shape[2]
    routed = row_count * top_count
    row_blocks, col_blocks = width // BLK, cols // BLK
    slots_each = fresh_codes.shape[2]
    some_unchanged = changed.shape[0] < experts

    gated = (hidden_act.astype(F32) * gates[..., None]).astype(BF16).reshape(step_count, routed, width)
    flat_routes = routes.reshape(step_count, routed)
    row = jnp.arange(experts * row_count, dtype=jnp.int32)
    entry = jnp.arange(routed, dtype=jnp.int32)

    def spread(step):
        pick = (row[:, None] // row_count == flat_routes[step][None, :]) & (
            row[:, None] % row_count == entry[None, :] // top_count
        )
        out = jnp.dot(pick.astype(BF16), gated[step], preferred_element_type=F32)
        return out.astype(BF16).reshape(experts, row_count, width)

    def with_routes(step):
        tail = jnp.zeros((PAD_ROWS, width), BF16).at[0, :routed].set(flat_routes[step].astype(BF16))
        return jnp.concatenate([gated[step], tail], axis=0)

    codes = fresh_codes.reshape((-1, BLK, BLK))
    scales = down_scales[0]

    third = 2 * (col_blocks // 6)
    part_blocks = (col_blocks - 2 * third, third, third)

    def fresh_order(changed, block_ids, fresh_scales):
        first = own * slots_each
        own_ids = lax.dynamic_slice_in_dim(block_ids[:, own_half], first, slots_each, axis=1)
        return fresh_plan(own_ids, fresh_scales[:, 0], changed, col_blocks, row_blocks)

    def old(act, order):
        return old_product(act, down_codes[0], scales, order)

    def fresh(pieces, pos, plan):
        return fresh_product(pieces, pos, codes, plan, part_blocks, experts, row_count, top_count)

    if experts == ChipGrid.SIZE and learners == 1 and not some_unchanged and step_count == 2:
        grid = ChipGrid()
        together = lax.optimization_barrier
        order = jnp.asarray(grid.rank_source)[own]
        pos = jnp.asarray(grid.piece_rank)[own]
        unit = row_count

        spread_old, first_piece = prepare(hidden_act, routes, gates, experts)
        p = [first_piece]
        p.append(grid.hop(p[0]))
        q = [grid.other_core(p[0])]
        q[0], spread_old = together((q[0], spread_old))
        q.append(grid.hop(q[0]))
        act_old = lax.all_to_all(spread_old, "expert", split_axis=0, concat_axis=0, tiled=True)
        q[1], order, pos, changed, block_ids, fresh_scales = together(
            (q[1], order, pos, changed, block_ids, fresh_scales)
        )
        plan = fresh_order(changed, block_ids, fresh_scales)

        p.append(grid.hop(p[1]))
        q.append(grid.hop(q[1]))
        q[2], act_old, plan = together((q[2], act_old, plan))

        p.append(grid.hop(p[2]))
        q.append(grid.hop(q[2]))
        keep_old, send_old = old(act_old, order)
        p[3], q[3], keep_old, send_old = together((p[3], q[3], keep_old, send_old))

        p.append(grid.hop(p[3]))
        got_old = grid.other_core(send_old)
        pieces = [p[0], q[0]]
        for k in (1, 2, 3):
            pieces += [p[k], q[k], grid.other_core(p[k]), grid.other_core(q[k])]

        cut = cols // 2 // BLK * BLK
        rows_y = add_cols(4 * unit, 8 * unit, 0, cut, keep_old, got_old)
        rows_z = jnp.concatenate(
            [add_cols(first, first + 2 * unit, cut, cols, keep_old, got_old) for first in (2 * unit, 6 * unit)]
        )
        pieces, rows_y, rows_z = together((pieces, rows_y, rows_z))
        pieces += [p[4], grid.other_core(p[4])]

        old_y = grid.other_y(rows_y)
        old_z = grid.near_z(rows_z)
        halves = fresh(pieces, pos, plan)
        old_y, old_z, halves = together((old_y, old_z, halves))

        terms = [[keep, grid.other_core(send)] for keep, send in halves]
        for term in terms:
            term.append(grid.other_y(add_rows(4 * unit, 8 * unit, *term)))
        y_terms = [keep_old[: 4 * unit, :cut], got_old[: 4 * unit, :cut], old_y]
        z_terms = [
            jnp.concatenate([term[: 2 * unit, cut:], term[4 * unit : 6 * unit, cut:]]) for term in (keep_old, got_old)
        ] + [old_z]
        near_y = grid.near_z(add_rows(2 * unit, 4 * unit, *y_terms))
        far_z = jnp.concatenate([add_rows(first, first + unit, *z_terms) for first in (unit, 3 * unit)])
        far_z = grid.far_z(far_z)
        terms[0][2], near_y, far_z = together((terms[0][2], near_y, far_z))

        y_terms = [term[: 2 * unit] for term in y_terms] + [near_y]
        z_terms = [jnp.concatenate([term[:unit], term[2 * unit : 3 * unit]]) for term in z_terms] + [far_z]
        end_y = grid.far_z(add_rows(unit, 2 * unit, *y_terms))
        end_z = grid.other_y(add_rows(unit, 2 * unit, *z_terms))
        ends = {}
        parts = len(terms)
        for phase in range(parts + 1):
            moving = {}
            if phase < parts:
                moving["near"] = grid.near_z(add_rows(2 * unit, 4 * unit, *terms[phase]))
            if phase >= 1:
                last = [term[: 2 * unit] for term in terms[phase - 1]]
                moving["end"] = grid.far_z(add_rows(unit, 2 * unit, *last))
            if phase + 1 < parts:
                moving["y"] = terms[phase + 1][2]
            if phase == 0:
                moving["old"] = (end_y, end_z)
            moving = together(moving)
            if phase < parts:
                terms[phase].append(moving["near"])
            if phase >= 1:
                ends[phase - 1] = moving["end"]
            if phase + 1 < parts:
                terms[phase + 1][2] = moving["y"]
            if phase == 0:
                end_y, end_z = moving["old"]
        old_out = [add_rows(0, unit, *y_terms, end_y), add_rows(0, unit, *z_terms, end_z)]
        new_out = [add_rows(0, unit, *terms[i], ends[i]) for i in range(parts)]
        return jnp.stack([jnp.concatenate(old_out, axis=1), jnp.concatenate(new_out, axis=1)])

    group = experts * learners
    straight = jnp.arange(group, dtype=jnp.int32)

    def joined(halves):
        return jnp.concatenate([jnp.concatenate(half, axis=0) for half in halves], axis=1)

    def combine(part):
        summed = lax.psum_scatter(part, "expert", scatter_dimension=0, tiled=True)
        return lax.all_to_all(summed, "learner", split_axis=0, concat_axis=1, tiled=True)

    def old_part(step):
        dense = lax.all_to_all(spread(step), "expert", split_axis=0, concat_axis=0, tiled=True)
        if step > 0:
            dense = jnp.where(jnp.any(changed == own), jnp.zeros_like(dense), dense)
        dense = lax.all_gather(dense, "learner", axis=1, tiled=False)
        dense = dense.reshape(group, row_count, width)
        chunks = []
        for first in range(0, group, at_once):
            act = dense[first : first + at_once]
            chunks.append(joined([old(act, straight[:at_once])]))
        return jnp.concatenate(chunks, axis=0)

    def fresh_part(step):
        everyone = lax.all_gather(with_routes(step), ("expert", "learner"), axis=0)
        chunks = []
        for first in range(0, group, at_once):
            pieces = [everyone[first + i] for i in range(at_once)]
            chunks.append(joined(fresh(pieces, straight[:at_once], plan)))
        return jnp.concatenate(chunks, axis=0)

    at_once = min(group, 16)
    plan = fresh_order(changed, block_ids, fresh_scales)
    results = [combine(old_part(0))]
    for step in range(1, step_count):
        total = fresh_part(step)
        if some_unchanged:
            total = add(total, old_part(step))
        results.append(combine(total))
    return jnp.stack(results)


def solution(mesh):
    in_specs = (
        P(None, ("groups", "expert", "learner"), None, None),
        P(None, ("groups", "expert", "learner"), None),
        P(None, ("groups", "expert", "learner"), None),
        P("expert", None, "learner"),
        P("expert", None, "learner"),
        P("groups"),
        P("groups", "learner", "expert", None, None),
        P("groups", "learner", "expert"),
        P("groups", None, None),
    )
    out_specs = P(None, ("groups", "expert", "learner"), None)
    return jax.shard_map(body, mesh=mesh, in_specs=in_specs, out_specs=out_specs, check_vma=False)
```

```python
import functools

import jax
import jax.numpy as jnp
import numpy as np
from jax import lax
from jax.experimental import pallas as pl
from jax.experimental.pallas import tpu as pltpu
from jax.sharding import PartitionSpec as P

BLK = 128
LANES = 128
PAD_ROWS = 16
PAIRS = 24
SPARE_VMEM = 8 * 1024 * 1024
F32 = jnp.float32
BF16 = jnp.bfloat16


def in_vmem(x):
    return pltpu.with_memory_space_constraint(x, pltpu.VMEM)


def in_hbm(x):
    return pltpu.with_memory_space_constraint(x, pltpu.HBM)


def prepare_kernel(experts, act_hbm, route_hbm, gate_hbm, spread_ref, piece_ref, act_ref, route_ref, gate_ref, sems):
    _, top_count, row_count = gate_ref.shape
    width = act_ref.shape[1]
    routed = row_count * top_count
    arrivals = [
        pltpu.make_async_copy(source, here, sems.at[i])
        for i, (source, here) in enumerate(((act_hbm, act_ref), (route_hbm, route_ref), (gate_hbm, gate_ref)))
    ]
    for arrival in arrivals:
        arrival.start()
    for arrival in arrivals:
        arrival.wait()
    choice = lax.broadcasted_iota(jnp.int32, (top_count, routed), 0)
    entry = lax.broadcasted_iota(jnp.int32, (top_count, routed), 1)

    def gated(step):
        gate = jnp.concatenate([gate_ref[step][:, r : r + 1] for r in range(row_count)], axis=0)
        return (act_ref[step * routed : (step + 1) * routed, :].astype(F32) * gate).astype(BF16)

    def route_row(step):
        routes = route_ref[step].astype(F32)
        wide = jnp.zeros((top_count, routed), F32)
        for r in range(row_count):
            wide = jnp.where(entry // top_count == r, routes[:, r : r + 1], wide)
        return jnp.sum(jnp.where(entry % top_count == choice, wide, 0.0), axis=0, keepdims=True)

    piece_ref[0:routed, :] = gated(1)
    piece_ref[routed:, :] = jnp.zeros((PAD_ROWS, width), BF16)
    top = lax.broadcasted_iota(jnp.int32, (PAD_ROWS, routed), 0) == 0
    piece_ref[routed:, 0:routed] = jnp.where(top, route_row(1), 0.0).astype(BF16)
    long_row = lax.broadcasted_iota(jnp.int32, (experts * row_count, routed), 0)
    long_entry = lax.broadcasted_iota(jnp.int32, (experts * row_count, routed), 1)
    match = (long_row % row_count == long_entry // top_count) & (
        (long_row // row_count).astype(F32) == route_row(0)
    )
    pick = jnp.where(match, 1.0, 0.0).astype(BF16)
    spread = jnp.dot(pick, gated(0), preferred_element_type=F32).astype(BF16)
    for e in range(experts):
        spread_ref[e] = spread[e * row_count : (e + 1) * row_count]


def prepare(hidden_act, routes, gates, experts):
    _, row_count, top_count, width = hidden_act.shape
    whole = pl.BlockSpec(memory_space=pltpu.VMEM)
    return pl.pallas_call(
        functools.partial(prepare_kernel, experts),
        in_specs=[pl.BlockSpec(memory_space=pl.ANY)] * 3,
        out_specs=[whole] * 2,
        scratch_shapes=[
            pltpu.VMEM((2 * row_count * top_count, width), BF16),
            pltpu.VMEM((2, top_count, row_count), jnp.int32),
            pltpu.VMEM((2, top_count, row_count), F32),
            pltpu.SemaphoreType.DMA((3,)),
        ],
        out_shape=[
            pltpu.VMEM((experts, row_count, width), BF16),
            pltpu.VMEM((row_count * top_count + PAD_ROWS, width), BF16),
        ],
        compiler_params=pltpu.CompilerParams(vmem_limit_bytes=2 * SPARE_VMEM),
        cost_estimate=pl.CostEstimate(flops=0, bytes_accessed=0, transcendentals=0),
        name="prepare",
    )(*[in_hbm(x) for x in (hidden_act.reshape(-1, width), routes.transpose(0, 2, 1), gates.transpose(0, 2, 1))])


def old_kernel(order_ref, scale_ref, act_ref, code_hbm, keep_ref, send_ref, act_scratch, code_buf, code_sem):
    groups, group_rows, width = act_ref.shape
    chunks, _, chunk_cols = code_buf.shape

    def arrival(c):
        columns = pl.ds(c * chunk_cols, chunk_cols)
        return pltpu.make_async_copy(code_hbm.at[:, columns], code_buf.at[c], code_sem.at[c])

    for c in range(chunks):
        arrival(c).start()
    for g in range(groups):
        act_scratch[g * group_rows : (g + 1) * group_rows, :] = act_ref[order_ref[g]]
    act = act_scratch[...]
    half = act.shape[0] // 2
    per_chunk = chunk_cols // BLK
    for c in range(chunks):
        arrival(c).wait()
        for t in range(0, per_chunk, 2):
            rows = []
            for i in range(width // BLK):
                pair = []
                for j in range(t, t + 2):
                    block = code_buf[c, i * BLK : (i + 1) * BLK, j * BLK : (j + 1) * BLK]
                    scale = scale_ref[i * chunks * per_chunk + c * per_chunk + j]
                    pair.append((block.astype(F32) * scale).astype(BF16))
                rows.append(jnp.concatenate(pair, axis=1))
            weight = jnp.concatenate(rows, axis=0)
            product = jnp.dot(act, weight, preferred_element_type=F32).astype(BF16)
            at = slice(c * chunk_cols + t * BLK, c * chunk_cols + (t + 2) * BLK)
            keep_ref[:, at] = product[:half]
            send_ref[:, at] = product[half:]


def halves_of(rows, part_blocks):
    shapes = []
    for blocks in part_blocks:
        shapes += [pltpu.VMEM((rows // 2, blocks * BLK), BF16)] * 2
    return shapes


def old_product(act, codes, scales, order):
    groups, group_rows, width = act.shape
    rows, cols = groups * group_rows, codes.shape[1]
    chunks = cols // (14 * BLK)
    whole = pl.BlockSpec(memory_space=pltpu.VMEM)
    return pl.pallas_call(
        old_kernel,
        grid_spec=pltpu.PrefetchScalarGridSpec(
            num_scalar_prefetch=2,
            grid=(),
            in_specs=[whole, pl.BlockSpec(memory_space=pl.ANY)],
            out_specs=[whole] * 2,
            scratch_shapes=[
                pltpu.VMEM((rows, width), BF16),
                pltpu.VMEM((chunks, width, cols // chunks), BF16),
                pltpu.SemaphoreType.DMA((chunks,)),
            ],
        ),
        out_shape=halves_of(rows, (cols // BLK,)),
        compiler_params=pltpu.CompilerParams(vmem_limit_bytes=2 * (rows + cols) * width + SPARE_VMEM),
        cost_estimate=pl.CostEstimate(flops=0, bytes_accessed=0, transcendentals=0),
        name="old_product",
    )(order, scales.reshape(-1), in_vmem(act), in_hbm(codes))


def fresh_kernel(
    n_pieces, experts, row_count, top_count, part_blocks,
    pos_ref, steps_ref, column_ref, slot_ref, index_ref, scale_ref,
    *refs,
):
    pieces, code_ref = refs[:n_pieces], refs[n_pieces]
    outs, dense, total = refs[n_pieces + 1 : -2], refs[-2], refs[-1]
    width = pieces[0].shape[1]
    row_blocks = width // BLK
    routed = row_count * top_count
    slots = code_ref.shape[0]
    half = dense.shape[1] // 2

    row = lax.broadcasted_iota(jnp.int32, (experts * row_count, routed), 0)
    col = lax.broadcasted_iota(jnp.int32, (experts * row_count, routed), 1)
    same_row = row % row_count == col // top_count
    expert = (row // row_count).astype(F32)
    for i in range(n_pieces):
        route = pieces[i][routed : routed + PAD_ROWS, 0:routed].astype(F32)[0:1, :]
        pick = jnp.where(same_row & (expert == route), 1.0, 0.0).astype(BF16)
        spread = jnp.dot(pick, pieces[i][0:routed, :], preferred_element_type=F32).astype(BF16)
        at = pl.ds(pl.multiple_of(pos_ref[i] * row_count, row_count), row_count)
        for e in range(experts):
            for b in range(row_blocks):
                dense[e * row_blocks + b, at, :] = spread[
                    e * row_count : (e + 1) * row_count, b * BLK : (b + 1) * BLK
                ]

    def clear(j, carry):
        total[j] = jnp.zeros(total.shape[1:], F32)
        return carry

    def some_pairs(t, carry):
        products = []
        for u in range(PAIRS):
            number = t * PAIRS + u
            left, right = [], []
            for q in range(2):
                slot = slot_ref[2 * number + q]
                block = code_ref[jnp.minimum(slot, slots - 1)]
                right.append((block.astype(F32) * scale_ref[slot]).astype(BF16))
                left.append(dense[index_ref[slot]])
            left, right = jnp.concatenate(left, axis=1), jnp.concatenate(right, axis=0)
            products.append(jnp.dot(left, right, preferred_element_type=F32))
        for u in range(PAIRS):
            total[column_ref[t * PAIRS + u]] += products[u]
        return carry

    lax.fori_loop(0, total.shape[0], clear, 0)
    lax.fori_loop(0, steps_ref[0], some_pairs, 0)
    first = 0
    for part, blocks in enumerate(part_blocks):
        for j in range(blocks):
            done = total[first + j].astype(BF16)
            outs[2 * part][:, j * BLK : (j + 1) * BLK] = done[:half]
            outs[2 * part + 1][:, j * BLK : (j + 1) * BLK] = done[half:]
        first += blocks


def fresh_product(pieces, pos, codes, plan, part_blocks, experts, row_count, top_count):
    n_pieces = len(pieces)
    rows, cols = n_pieces * row_count, sum(part_blocks) * BLK
    width = pieces[0].shape[1]
    slots = codes.shape[0]
    whole = pl.BlockSpec(memory_space=pltpu.VMEM)
    outs = pl.pallas_call(
        functools.partial(fresh_kernel, n_pieces, experts, row_count, top_count, part_blocks),
        grid_spec=pltpu.PrefetchScalarGridSpec(
            num_scalar_prefetch=6,
            grid=(),
            in_specs=[whole] * (n_pieces + 1),
            out_specs=[whole] * (2 * len(part_blocks)),
            scratch_shapes=[
                pltpu.VMEM((experts * (width // BLK), rows, BLK), BF16),
                pltpu.VMEM((sum(part_blocks), rows, BLK), F32),
            ],
        ),
        out_shape=halves_of(rows, part_blocks),
        compiler_params=pltpu.CompilerParams(
            vmem_limit_bytes=2 * experts * width * rows + 4 * rows * cols + SPARE_VMEM
        ),
        cost_estimate=pl.CostEstimate(flops=0, bytes_accessed=0, transcendentals=0),
        name="fresh_product",
    )(pos, *plan, *[in_vmem(piece) for piece in pieces], in_vmem(codes))
    return [outs[2 * i : 2 * i + 2] for i in range(len(part_blocks))]


def fresh_plan(own_ids, own_scales, changed, col_blocks, row_blocks):
    slots_each = own_ids.shape[1]
    ids = own_ids.reshape(-1)
    count = ids.shape[0]
    column = ids % col_blocks
    index = jnp.repeat(changed, slots_each) * row_blocks + ids // col_blocks
    number = jnp.arange(count, dtype=jnp.int32)
    columns = jnp.arange(col_blocks, dtype=jnp.int32)
    most = -(-(count // 2 + (col_blocks + 1) // 2) // PAIRS) * PAIRS
    pairs = (jnp.sum((column[None, :] == columns[:, None]).astype(jnp.int32), axis=1) + 1) // 2
    before = jnp.sum(jnp.where(columns[None, :] < column[:, None], pairs[None, :], 0), axis=1)
    earlier = (column[None, :] == column[:, None]) & (number[None, :] < number[:, None])
    place = 2 * before + jnp.sum(earlier.astype(jnp.int32), axis=1)
    places = jnp.arange(2 * most, dtype=jnp.int32)
    slot = count - jnp.sum(jnp.where(place[None, :] == places[:, None], count - number[None, :], 0), axis=1)
    ends = jnp.sum(jnp.where(columns[None, :] <= columns[:, None], pairs[None, :], 0), axis=1)
    pair_column = jnp.sum((ends[None, :] <= places[:most, None]).astype(jnp.int32), axis=1)
    pair_column = jnp.minimum(pair_column, col_blocks - 1)
    steps = (ends[-1:] + PAIRS - 1) // PAIRS
    return steps, pair_column, slot, jnp.pad(index, (0, 1)), jnp.pad(own_scales.reshape(-1), (0, 1))


def add(*terms):
    total = terms[0].astype(F32)
    for term in terms[1:]:
        total = total + term.astype(F32)
    return total.astype(BF16)


class ChipGrid:
    SIZE = 16
    CYCLE = [(0, 0), (1, 0), (2, 0), (3, 0), (3, 1), (2, 1), (1, 1), (0, 1)]

    def __init__(self):
        cycle = self.CYCLE
        n = len(cycle)
        at = {chip: i for i, chip in enumerate(cycle)}
        number = lambda z, y, c: (z * 2 + y) * 2 + c
        self.ring = []
        self.piece_rank = np.zeros((self.SIZE, self.SIZE), np.int32)
        self.rank_source = np.zeros((self.SIZE, self.SIZE), np.int32)
        for z in range(4):
            for y in range(2):
                for c in range(2):
                    me, i = number(z, y, c), at[(z, y)]
                    way = 1 if c == 0 else -1
                    self.ring.append((me, number(*cycle[(i + way) % n], c)))
                    found = [(0, 0), (0, 1)]
                    for hop in (1, 2, 3):
                        found += [(-way * hop, 0), (-way * hop, 1), (way * hop, 1), (way * hop, 0)]
                    found += [(4, 0), (4, 1)]
                    for k, (offset, dc) in enumerate(found):
                        sz, sy = cycle[(i + offset) % n]
                        self.piece_rank[me, k] = self.rank(sz ^ z, sy ^ y, dc)
                    for dz in range(4):
                        for dy in range(2):
                            for dc in range(2):
                                self.rank_source[me, self.rank(dz, dy, dc)] = number(z ^ dz, y ^ dy, c ^ dc)

    @staticmethod
    def rank(dz, dy, dc):
        return dc * 8 + dy * 4 + (dz % 2) * 2 + dz // 2

    def partner(self, x, dz, dy, dc):
        delta = (dz * 2 + dy) * 2 + dc
        return lax.ppermute(x, "expert", [(i, i ^ delta) for i in range(self.SIZE)])

    def hop(self, x):
        return lax.ppermute(x, "expert", self.ring)

    def other_core(self, x):
        return self.partner(x, 0, 0, 1)

    def other_y(self, x):
        return self.partner(x, 0, 1, 0)

    def near_z(self, x):
        return self.partner(x, 1, 0, 0)

    def far_z(self, x):
        return self.partner(x, 2, 0, 0)


def add_rows(first, last, *terms):
    return add(*[term[first:last] for term in terms])


def add_cols(first, last, first_col, last_col, *terms):
    return add(*[term[first:last, first_col:last_col] for term in terms])


def body(
    hidden_act,
    routes,
    gates,
    down_codes,
    down_scales,
    changed,
    fresh_codes,
    fresh_scales,
    block_ids,
):
    experts = lax.axis_size("expert")
    learners = lax.axis_size("learner")
    own = lax.axis_index("expert")
    own_half = lax.axis_index("learner")
    step_count, row_count, top_count, width = hidden_act.shape
    cols = down_codes.shape[2]
    routed = row_count * top_count
    row_blocks, col_blocks = width // BLK, cols // BLK
    slots_each = fresh_codes.shape[2]
    some_unchanged = changed.shape[0] < experts

    gated = (hidden_act.astype(F32) * gates[..., None]).astype(BF16).reshape(step_count, routed, width)
    flat_routes = routes.reshape(step_count, routed)
    row = jnp.arange(experts * row_count, dtype=jnp.int32)
    entry = jnp.arange(routed, dtype=jnp.int32)

    def spread(step):
        pick = (row[:, None] // row_count == flat_routes[step][None, :]) & (
            row[:, None] % row_count == entry[None, :] // top_count
        )
        out = jnp.dot(pick.astype(BF16), gated[step], preferred_element_type=F32)
        return out.astype(BF16).reshape(experts, row_count, width)

    def with_routes(step):
        tail = jnp.zeros((PAD_ROWS, width), BF16).at[0, :routed].set(flat_routes[step].astype(BF16))
        return jnp.concatenate([gated[step], tail], axis=0)

    codes = fresh_codes.reshape((-1, BLK, BLK))
    scales = down_scales[0]

    third = 2 * (col_blocks // 6)
    part_blocks = (col_blocks - 2 * third, third, third)

    def fresh_order(changed, block_ids, fresh_scales):
        first = own * slots_each
        own_ids = lax.dynamic_slice_in_dim(block_ids[:, own_half], first, slots_each, axis=1)
        return fresh_plan(own_ids, fresh_scales[:, 0], changed, col_blocks, row_blocks)

    def old(act, order):
        return old_product(act, down_codes[0], scales, order)

    def fresh(pieces, pos, plan):
        return fresh_product(pieces, pos, codes, plan, part_blocks, experts, row_count, top_count)

    if experts == ChipGrid.SIZE and learners == 1 and not some_unchanged and step_count == 2:
        grid = ChipGrid()
        together = lax.optimization_barrier
        order = jnp.asarray(grid.rank_source)[own]
        pos = jnp.asarray(grid.piece_rank)[own]
        unit = row_count

        spread_old, first_piece = prepare(hidden_act, routes, gates, experts)
        p = [first_piece]
        p.append(grid.hop(p[0]))
        q = [grid.other_core(p[0])]
        q[0], spread_old = together((q[0], spread_old))
        q.append(grid.hop(q[0]))
        act_old = lax.all_to_all(spread_old, "expert", split_axis=0, concat_axis=0, tiled=True)
        q[1], order, pos, changed, block_ids, fresh_scales = together(
            (q[1], order, pos, changed, block_ids, fresh_scales)
        )
        plan = fresh_order(changed, block_ids, fresh_scales)

        p.append(grid.hop(p[1]))
        q.append(grid.hop(q[1]))
        q[2], act_old, plan = together((q[2], act_old, plan))

        p.append(grid.hop(p[2]))
        q.append(grid.hop(q[2]))
        keep_old, send_old = old(act_old, order)
        p[3], q[3], keep_old, send_old = together((p[3], q[3], keep_old, send_old))

        p.append(grid.hop(p[3]))
        got_old = grid.other_core(send_old)
        pieces = [p[0], q[0]]
        for k in (1, 2, 3):
            pieces += [p[k], q[k], grid.other_core(p[k]), grid.other_core(q[k])]

        cut = cols // 2 // BLK * BLK
        rows_y = add_cols(4 * unit, 8 * unit, 0, cut, keep_old, got_old)
        rows_z = jnp.concatenate(
            [add_cols(first, first + 2 * unit, cut, cols, keep_old, got_old) for first in (2 * unit, 6 * unit)]
        )
        pieces, rows_y, rows_z = together((pieces, rows_y, rows_z))
        pieces += [p[4], grid.other_core(p[4])]

        old_y = grid.other_y(rows_y)
        old_z = grid.near_z(rows_z)
        halves = fresh(pieces, pos, plan)
        old_y, old_z, halves = together((old_y, old_z, halves))

        terms = [[keep, grid.other_core(send)] for keep, send in halves]
        for term in terms:
            term.append(grid.other_y(add_rows(4 * unit, 8 * unit, *term)))
        y_terms = [keep_old[: 4 * unit, :cut], got_old[: 4 * unit, :cut], old_y]
        z_terms = [
            jnp.concatenate([term[: 2 * unit, cut:], term[4 * unit : 6 * unit, cut:]]) for term in (keep_old, got_old)
        ] + [old_z]
        near_y = grid.near_z(add_rows(2 * unit, 4 * unit, *y_terms))
        far_z = jnp.concatenate([add_rows(first, first + unit, *z_terms) for first in (unit, 3 * unit)])
        far_z = grid.far_z(far_z)
        terms[0][2], near_y, far_z = together((terms[0][2], near_y, far_z))

        y_terms = [term[: 2 * unit] for term in y_terms] + [near_y]
        z_terms = [jnp.concatenate([term[:unit], term[2 * unit : 3 * unit]]) for term in z_terms] + [far_z]
        end_y = grid.far_z(add_rows(unit, 2 * unit, *y_terms))
        end_z = grid.other_y(add_rows(unit, 2 * unit, *z_terms))
        ends = {}
        parts = len(terms)
        for phase in range(parts + 1):
            moving = {}
            if phase < parts:
                moving["near"] = grid.near_z(add_rows(2 * unit, 4 * unit, *terms[phase]))
            if phase >= 1:
                last = [term[: 2 * unit] for term in terms[phase - 1]]
                moving["end"] = grid.far_z(add_rows(unit, 2 * unit, *last))
            if phase + 1 < parts:
                moving["y"] = terms[phase + 1][2]
            if phase == 0:
                moving["old"] = (end_y, end_z)
            moving = together(moving)
            if phase < parts:
                terms[phase].append(moving["near"])
            if phase >= 1:
                ends[phase - 1] = moving["end"]
            if phase + 1 < parts:
                terms[phase + 1][2] = moving["y"]
            if phase == 0:
                end_y, end_z = moving["old"]
        old_out = [add_rows(0, unit, *y_terms, end_y), add_rows(0, unit, *z_terms, end_z)]
        new_out = [add_rows(0, unit, *terms[i], ends[i]) for i in range(parts)]
        return jnp.stack([jnp.concatenate(old_out, axis=1), jnp.concatenate(new_out, axis=1)])

    group = experts * learners
    straight = jnp.arange(group, dtype=jnp.int32)

    def joined(halves):
        return jnp.concatenate([jnp.concatenate(half, axis=0) for half in halves], axis=1)

    def combine(part):
        summed = lax.psum_scatter(part, "expert", scatter_dimension=0, tiled=True)
        return lax.all_to_all(summed, "learner", split_axis=0, concat_axis=1, tiled=True)

    def old_part(step):
        dense = lax.all_to_all(spread(step), "expert", split_axis=0, concat_axis=0, tiled=True)
        if step > 0:
            dense = jnp.where(jnp.any(changed == own), jnp.zeros_like(dense), dense)
        dense = lax.all_gather(dense, "learner", axis=1, tiled=False)
        dense = dense.reshape(group, row_count, width)
        chunks = []
        for first in range(0, group, at_once):
            act = dense[first : first + at_once]
            chunks.append(joined([old(act, straight[:at_once])]))
        return jnp.concatenate(chunks, axis=0)

    def fresh_part(step):
        everyone = lax.all_gather(with_routes(step), ("expert", "learner"), axis=0)
        chunks = []
        for first in range(0, group, at_once):
            pieces = [everyone[first + i] for i in range(at_once)]
            chunks.append(joined(fresh(pieces, straight[:at_once], plan)))
        return jnp.concatenate(chunks, axis=0)

    at_once = min(group, 16)
    plan = fresh_order(changed, block_ids, fresh_scales)
    results = [combine(old_part(0))]
    for step in range(1, step_count):
        total = fresh_part(step)
        if some_unchanged:
            total = add(total, old_part(step))
        results.append(combine(total))
    return jnp.stack(results)


def solution(mesh):
    in_specs = (
        P(None, ("groups", "expert", "learner"), None, None),
        P(None, ("groups", "expert", "learner"), None),
        P(None, ("groups", "expert", "learner"), None),
        P("expert", None, "learner"),
        P("expert", None, "learner"),
        P("groups"),
        P("groups", "learner", "expert", None, None),
        P("groups", "learner", "expert"),
        P("groups", None, None),
    )
    out_specs = P(None, ("groups", "expert", "learner"), None)
    return jax.shard_map(body, mesh=mesh, in_specs=in_specs, out_specs=out_specs, check_vma=False)
```
